32 devices in a mesh: ctx: 8 (over y, x, core), head: 4 (over z).
Axes of the slice: x: 2, y: 2, z: 4, core: 2. Of those that a mesh axis runs over, the one named last changes fastest.
Arguments:
- queries: bfloat16 [2048, 4096], P('ctx', 'head'), may hold values from -100 to 100
- keys: bfloat16 [16384, 4096], P('ctx', 'head'), may hold values from -4 to 4
- values: bfloat16 [16384, 4096], P('ctx', 'head'), may hold values from -6 to 6
- lengths: int32 [64], P('ctx'), may hold values from 1 to 256, as said below
- out_weight: bfloat16 [4096, 4096], P('head'), may hold values from -0.09375 to 0.09375
Outputs:
- layer_out: float32 [2048, 4096], P('ctx', 'head')
The draws below stay inside these ranges and needn't reach their ends.
Inputs may be any that keep to these rules, and one draw needn't show every extreme that they name: `lengths`: each passage has at least one valid token; some passage is full and some has exactly one.
All inputs are finite; a program needn't handle non-finite values.
Results may differ from the reference program's by a relative error of at most 0.005.
Values may be sent and summed in bfloat16 or wider, within the bound.
No kernel may reach another device: no remote copies, remote signals or barrier semaphores. Data moves between devices by JAX's collectives and lax.ppermute only.
A program may use at most 192 MiB of HBM per device.

```python
import math
import jax
import jax.numpy as jnp
from jax import lax

D = 4096
HEADS = 32
HD = 128
SPAN = 256
QROWS = 2048
CTX = 16384
NCHUNK = 64


def base_keys(key):
    drawn = jax.random.normal(jax.random.fold_in(key, 101), (CTX, HEADS * HD), jnp.float32)
    return jnp.clip(drawn, -4.0, 4.0)


def draw_keys(key, part):
    shared = base_keys(key)
    return shared.astype(jnp.bfloat16)


def draw_queries(key, part):
    key = jax.random.fold_in(key, 2)
    drawn_rows = jnp.clip(jax.random.normal(key, (QROWS, HEADS * HD), jnp.float32), -4.0, 4.0) * 3.0
    return drawn_rows.astype(jnp.bfloat16)


def draw_lengths(key, part):
    key = jax.random.fold_in(key, 3)
    length_key, order_key = jax.random.split(key)
    valid_lengths = jax.random.randint(length_key, (NCHUNK,), 1, SPAN + 1, jnp.int32)
    order = jax.random.permutation(order_key, NCHUNK)
    valid_lengths = valid_lengths.at[order[0]].set(SPAN)
    valid_lengths = valid_lengths.at[order[1]].set(1)
    return valid_lengths.astype(jnp.int32)


def levels(stream_key, shape, cuts, least, largest):
    loudness = 1.0
    for dim, parts in cuts:
        steps = jax.random.uniform(jax.random.fold_in(jax.random.fold_in(stream_key, 6), dim), (parts,), jnp.float32, least / len(cuts), largest / len(cuts))
        loudness = loudness * jnp.repeat(jnp.exp(steps), shape[dim] // parts).reshape((-1,) + (1,) * (len(shape) - 1 - dim))
    return loudness


def normal_values(own_key, dims, scale, most, cuts=(), kind=jnp.bfloat16):
    values = jax.random.normal(own_key, dims, jnp.float32) * scale
    if len(cuts) > 0:
        values = levels(own_key, dims, cuts, -0.22, 0.18) * values
    return jnp.clip(values, min=-most, max=most).astype(kind)


def setup_inputs(seed: int = 0) -> dict:
    arg_keys = jax.random.split(jax.random.key(seed), 6)
    queries = draw_queries(jax.random.fold_in(arg_keys[5], 71), 0)
    keys = draw_keys(jax.random.fold_in(arg_keys[5], 71), 0)
    values = normal_values(arg_keys[2], (CTX, HEADS * HD), 1.0, 6.0, ((0, 8), (1, 4)))
    lengths = draw_lengths(jax.random.fold_in(arg_keys[5], 71), 0)
    out_weight = normal_values(arg_keys[4], (HEADS * HD, D), (HEADS * HD) ** -0.5, 0.09375, ((0, 4),))
    return dict(queries=queries, keys=keys, values=values, lengths=lengths, out_weight=out_weight)


def reference(queries, keys, values, lengths, out_weight):
    positions = jnp.arange(CTX, dtype=jnp.int32)
    limits = jnp.repeat(lengths, SPAN, total_repeat_length=CTX)
    mask_bias = jnp.where(positions % SPAN < limits, 0.0, -1e+30).astype(jnp.float32)
    score_scale = 1.0 / math.sqrt(HD)
    query_heads = queries.reshape(QROWS, HEADS, HD).transpose(1, 0, 2)
    key_heads = keys.reshape(CTX, HEADS, HD).transpose(1, 0, 2)
    value_heads = values.reshape(CTX, HEADS, HD).transpose(1, 0, 2)
    row_block = min(256, QROWS)

    def one_head(operands):
        query_one, key_one, value_one = operands

        def one_block(query_rows):
            scores = jnp.dot(query_rows, key_one.T, preferred_element_type=jnp.float32) * score_scale + mask_bias[None, :]
            row_max = lax.optimization_barrier(jnp.max(scores, axis=1, keepdims=True))
            raised = jnp.exp(scores - row_max)
            totals = lax.optimization_barrier(jnp.sum(raised, axis=1, keepdims=True))
            weighted = jnp.dot(raised.astype(jnp.bfloat16), value_one, preferred_element_type=jnp.float32)
            return (weighted / totals).astype(jnp.bfloat16)
        row_blocks = query_one.reshape(QROWS // row_block, row_block, HD)
        return lax.map(one_block, row_blocks).reshape(QROWS, HD)
    attended = lax.map(one_head, (query_heads, key_heads, value_heads))
    attended = attended.transpose(1, 0, 2).reshape(QROWS, HEADS * HD)
    return jnp.dot(attended, out_weight, preferred_element_type=jnp.float32)
```

```python
import functools
import math

import jax
import jax.numpy as jnp
from jax import lax
from jax.experimental import pallas as pl
from jax.experimental.pallas import tpu as pltpu
from jax.sharding import PartitionSpec as P

HD = 128
SPAN = 256
STEP = 16
BLOCK = 512
SUB = 256
CHUNKS = 2
STATS = 16
SCALE = math.log2(math.e) / math.sqrt(HD)
NT = (((1,), (1,)), ((), ()))
NN = (((1,), (0,)), ((), ()))
MIB = 2**20


def compact_kernel(spans, meta, own_k, own_v, got_k, got_v, out_k, out_v, out_m):
    head = pl.program_id(0)
    rows = lax.broadcasted_iota(jnp.int32, (SPAN, HD), 0)
    here = own_k.shape[0] // SPAN
    at = jnp.int32(0)
    for passage in range(2 * here):
        source_k, source_v = (own_k, own_v) if passage < here else (got_k, got_v)
        part = pl.ds((passage % here) * SPAN, SPAN)
        size = spans[passage]
        valid = rows < size
        k = source_k[part, :].astype(jnp.float32)
        v = source_v[part, :].astype(jnp.float32)
        first = jnp.broadcast_to(k[:1, :], k.shape)
        place = pl.ds(pl.multiple_of(at, STEP), SPAN)
        out_k[place, :] = jnp.where(valid, k, first).astype(jnp.bfloat16)
        out_v[place, :] = jnp.where(valid, v, 0.0).astype(jnp.bfloat16)

        @pl.when(head == 0)
        def _():
            out_m[place, :] = jnp.where(valid, 1.0, 0.0).astype(jnp.bfloat16)

        at = at + (size + STEP - 1) // STEP * STEP
    for extra in range(BLOCK // SPAN):
        place = pl.ds(pl.multiple_of(at + extra * SPAN, STEP), SPAN)
        out_k[place, :] = first.astype(jnp.bfloat16)
        out_v[place, :] = jnp.zeros((SPAN, HD), jnp.bfloat16)

        @pl.when(head == 0)
        def _():
            out_m[place, :] = jnp.zeros((SPAN, HD), jnp.bfloat16)


def compact(spans, core, keys, values, got_k, got_v):
    tokens, width = got_k.shape
    heads = width // HD
    size = 2 * tokens + BLOCK
    own = pl.BlockSpec((tokens, HD), lambda h, s, m: (0, m[0] * heads + h))
    got = pl.BlockSpec((tokens, HD), lambda h, s, m: (0, h))
    out = pl.BlockSpec((size, HD), lambda h, s, m: (0, h))
    return pl.pallas_call(
        compact_kernel,
        grid_spec=pltpu.PrefetchScalarGridSpec(
            num_scalar_prefetch=2,
            grid=(heads,),
            in_specs=[own, own, got, got],
            out_specs=[out, out, pl.BlockSpec((size, HD), lambda h, s, m: (0, 0))],
        ),
        out_shape=[
            jax.ShapeDtypeStruct((size, width), jnp.bfloat16),
            jax.ShapeDtypeStruct((size, width), jnp.bfloat16),
            jax.ShapeDtypeStruct((size, HD), jnp.bfloat16),
        ],
        compiler_params=pltpu.CompilerParams(vmem_limit_bytes=40 * MIB),
        cost_estimate=pl.CostEstimate(
            flops=0, bytes_accessed=8 * width * size, transcendentals=0
        ),
        name="compact",
    )(spans, core, keys, values, got_k, got_v)


def attend_kernel(blocks, tiles, count, *refs):
    q_refs, (k_ref, v_ref, m_ref) = refs[:blocks], refs[blocks : blocks + 3]
    o_refs = refs[blocks + 3 : 2 * blocks + 3]
    q_all, s_even, s_odd, top_even, top_odd, acc = refs[2 * blocks + 3 :]
    rows = q_refs[0].shape[0]
    step = pl.program_id(0)
    turns = (count[0] + BLOCK - 1) // BLOCK
    total = blocks * rows
    sub = min(SUB, total)

    def score(at, scores, top, part):
        s = lax.dot_general(
            q_all[part, :], k_ref[at, :], NT, preferred_element_type=jnp.float32
        )
        scores[part, at] = s
        most = top[part, :]
        for i in range(BLOCK // HD):
            most = jnp.maximum(most, s[:, i * HD : (i + 1) * HD])
        top[part, :] = most

    def weigh(at, scores, top, part):
        value = jnp.concatenate([v_ref[at, :], m_ref[at, :]], axis=1)
        most = top[part, :]
        s = scores[part, at]
        weights = jnp.concatenate(
            [
                jnp.exp2((s[:, i * HD : (i + 1) * HD] - most) * SCALE).astype(jnp.bfloat16)
                for i in range(BLOCK // HD)
            ],
            axis=1,
        )
        acc[part, :] += lax.dot_general(
            weights, value, NN, preferred_element_type=jnp.float32
        )

    def run(now, then):
        if then is not None:
            scores_then, top_then = then
            top_then[...] = jnp.broadcast_to(
                jnp.max(top_then[...], axis=1, keepdims=True), top_then.shape
            )
            acc[...] = jnp.zeros_like(acc)
        if now is not None:
            scores_now, top_now = now
            top_now[...] = jnp.full(top_now.shape, -3e38, jnp.float32)
            for b in range(blocks):
                q_all[b * rows : (b + 1) * rows, :] = q_refs[b][...]

        def body(turn, carry):
            at = pl.ds(pl.multiple_of(turn * BLOCK, BLOCK), BLOCK)
            for r in range(total // sub):
                part = pl.ds(r * sub, sub)
                if now is not None:
                    score(at, scores_now, top_now, part)
                if then is not None:
                    weigh(at, scores_then, top_then, part)
            return carry

        lax.fori_loop(0, turns, body, 0)
        if then is not None:
            for b in range(blocks):
                finish(b, top_then)

    def finish(b, top):
        group = min(rows, HD)
        for u in range(rows // group):
            part = pl.ds(b * rows + u * group, group)
            sums = acc[part, HD:]
            o_refs[b][u * group : (u + 1) * group, :] = (acc[part, :HD] / sums).astype(
                jnp.bfloat16
            )
            logs = top[part, :] * SCALE + jnp.log2(sums)
            eye = lax.broadcasted_iota(jnp.int32, (group, HD), 0) == (
                lax.broadcasted_iota(jnp.int32, (group, HD), 1)
            )
            line = jnp.sum(jnp.where(eye, logs, 0.0), axis=0, keepdims=True)
            high = line.astype(jnp.bfloat16).astype(jnp.float32)
            middle = (line - high).astype(jnp.bfloat16).astype(jnp.float32)
            low = line - high - middle
            index = lax.broadcasted_iota(jnp.int32, (STATS, HD), 0)
            packed = jnp.where(
                index == 0,
                high,
                jnp.where(index == 1, middle, jnp.where(index == 2, low, 0.0)),
            )
            o_refs[b][rows + u * STATS : rows + (u + 1) * STATS, :] = packed.astype(
                jnp.bfloat16
            )

    even, odd = (s_even, top_even), (s_odd, top_odd)
    is_even = lax.rem(step, 2) == 0
    inside = jnp.logical_and(step > 0, step < tiles)

    @pl.when(step == 0)
    def _():
        run(even, None)

    if tiles > 1:

        @pl.when(jnp.logical_and(inside, is_even))
        def _():
            run(even, odd)

        @pl.when(jnp.logical_and(inside, jnp.logical_not(is_even)))
        def _():
            run(odd, even)

    @pl.when(step == tiles)
    def _():
        run(None, odd if tiles % 2 == 0 else even)


def stat_rows(rows):
    return STATS * (rows // min(rows, HD))


def attend(count, queries, chunk, key, value, mark):
    blocks = len(queries)
    rows = queries[0].shape[0] // CHUNKS
    width = queries[0].shape[1]
    heads = width // HD
    size = key.shape[0]
    tall = rows + stat_rows(rows)
    now = lambda t: jnp.minimum(t, heads - 1)
    then = lambda t: jnp.maximum(t - 1, 0)
    total = blocks * rows
    return pl.pallas_call(
        functools.partial(attend_kernel, blocks, heads),
        grid_spec=pltpu.PrefetchScalarGridSpec(
            num_scalar_prefetch=1,
            grid=(heads + 1,),
            in_specs=[pl.BlockSpec((rows, HD), lambda t, n: (chunk, now(t)))] * blocks
            + [
                pl.BlockSpec((size, HD), lambda t, n: (0, now(t))),
                pl.BlockSpec((size, HD), lambda t, n: (0, then(t))),
                pl.BlockSpec((size, HD), lambda t, n: (0, 0)),
            ],
            out_specs=[pl.BlockSpec((tall, HD), lambda t, n: (0, then(t)))] * blocks,
            scratch_shapes=[
                pltpu.VMEM((total, HD), jnp.bfloat16),
                pltpu.VMEM((total, size), jnp.float32),
                pltpu.VMEM((total, size), jnp.float32),
                pltpu.VMEM((total, HD), jnp.float32),
                pltpu.VMEM((total, HD), jnp.float32),
                pltpu.VMEM((total, 2 * HD), jnp.float32),
            ],
        ),
        out_shape=[jax.ShapeDtypeStruct((tall, width), jnp.bfloat16)] * blocks,
        compiler_params=pltpu.CompilerParams(vmem_limit_bytes=58 * MIB),
        cost_estimate=pl.CostEstimate(
            flops=8 * total * size * width // 2, bytes_accessed=4 * size * width, transcendentals=0
        ),
        name="attend",
    )(count, *queries, key, value, mark)


def project_kernel(sources, order, meta, *refs):
    parts, weight = refs[: 2 * sources], refs[2 * sources]
    outs, attended = refs[2 * sources + 1 : -1], refs[-1]
    step = pl.program_id(0)
    rows = outs[0].shape[0]
    width = parts[0].shape[1]
    group = min(rows, HD)

    @pl.when(step == 0)
    def _():
        eye = lax.broadcasted_iota(jnp.int32, (group, HD), 0) == (
            lax.broadcasted_iota(jnp.int32, (group, HD), 1)
        )
        for side in range(2):
            mine = parts[side * sources : (side + 1) * sources]
            core = meta[0] if side == 0 else 1 - meta[0]
            for u in range(rows // group):
                there = slice(u * group, (u + 1) * group)
                for head in range(width // HD):
                    cols = slice(head * HD, (head + 1) * HD)
                    logs = []
                    for part in mine:
                        stats = part[rows + u * STATS : rows + (u + 1) * STATS, cols]
                        stats = stats.astype(jnp.float32)
                        logs.append(stats[0:1] + (stats[1:2] + stats[2:3]))
                    most = functools.reduce(jnp.maximum, logs)
                    shares = [jnp.exp2(x - most) for x in logs]
                    whole = functools.reduce(jnp.add, shares)
                    merged = None
                    for part, share in zip(mine, shares):
                        line = jnp.broadcast_to(share / whole, (group, HD))
                        column = jnp.sum(jnp.where(eye, line, 0.0), axis=1, keepdims=True)
                        term = part[there, cols].astype(jnp.float32) * column
                        merged = term if merged is None else merged + term
                    place = pl.ds(pl.multiple_of(core * width + head * HD, HD), HD)
                    attended[there, place] = merged.astype(jnp.bfloat16)

    for i in range(len(outs)):

        @pl.when(step == i)
        def _(i=i):
            outs[i][...] = lax.dot_general(
                attended[...], weight[...], NN, preferred_element_type=jnp.float32
            ).astype(outs[i].dtype)


def project(meta, own, other, out_weight, groups, rows):
    depth, total = out_weight.shape
    cols = total // groups
    sources = len(own)
    whole = pl.BlockSpec(own[0].shape, lambda t, m: (0, 0))
    order = [d for d in range(groups - 1, 0, -1)] + [0]
    return pl.pallas_call(
        functools.partial(project_kernel, sources, order),
        grid_spec=pltpu.PrefetchScalarGridSpec(
            num_scalar_prefetch=1,
            grid=(groups,),
            in_specs=[whole] * (2 * sources)
            + [pl.BlockSpec((depth, cols), lambda t, m: (0, m[1] ^ (groups - 1 - t)))],
            out_specs=[pl.BlockSpec((rows, cols), lambda t, m: (0, 0))] * groups,
            scratch_shapes=[pltpu.VMEM((rows, depth), jnp.bfloat16)],
        ),
        out_shape=[
            jax.ShapeDtypeStruct((rows, cols), jnp.bfloat16 if d else jnp.float32)
            for d in order
        ],
        compiler_params=pltpu.CompilerParams(vmem_limit_bytes=40 * MIB),
        cost_estimate=pl.CostEstimate(
            flops=2 * rows * depth * total, bytes_accessed=2 * depth * total, transcendentals=0
        ),
        name="project",
    )(meta, *own, *other, out_weight)


def on_device(queries, keys, values, lengths, out_weight):
    sources = lax.axis_size("ctx")
    groups = lax.axis_size("head")
    core = lax.rem(lax.axis_index("ctx"), 2)
    width = keys.shape[1] // 2
    meta = jnp.stack([core, lax.axis_index("head")]).astype(jnp.int32)

    def swap(x, k, axis="ctx"):
        n = sources if axis == "ctx" else groups
        return lax.ppermute(x, axis, [(i, i ^ k) for i in range(n)])

    def half(x, which):
        return lax.dynamic_slice(x, (0, which * width), (x.shape[0], width))

    got_k = swap(half(keys, 1 - core), 1)
    got_v = swap(half(values, 1 - core), 1)
    spans = jnp.concatenate([lengths, swap(lengths, 1)])
    count = jnp.sum((spans + STEP - 1) // STEP * STEP).reshape(1)
    mine, others = half(queries, core), half(queries, 1 - core)
    asked = [mine] + [swap(mine if k % 2 == 0 else others, k) for k in range(1, sources)]
    key, value, mark = compact(spans, meta, keys, values, got_k, got_v)

    rows = queries.shape[0] // CHUNKS
    outs = []
    for chunk in range(CHUNKS):
        partial = attend(count, asked, chunk, key, value, mark)
        back = [partial[0]] + [swap(partial[k], k) for k in range(1, sources)]
        blocks = project(meta, back[0::2], back[1::2], out_weight, groups, rows)
        total = blocks[-1]
        for d in range(groups - 1, 0, -1):
            total = total + swap(blocks[groups - 1 - d], d, "head").astype(jnp.float32)
        outs.append(total)
    return jnp.concatenate(outs, axis=0)


def solution(mesh):
    in_specs = (P("ctx", "head"), P("ctx", "head"), P("ctx", "head"), P("ctx"), P("head", None))
    out_specs = P("ctx", "head")
    return jax.shard_map(
        on_device, mesh=mesh, in_specs=in_specs, out_specs=out_specs, check_vma=False
    )
```

```python
import functools
import math

import jax
import jax.numpy as jnp
from jax import lax
from jax.experimental import pallas as pl
from jax.experimental.pallas import tpu as pltpu
from jax.sharding import PartitionSpec as P

HD = 128
SPAN = 256
STEP = 16
UNIT = 256
BLOCK = 4 * UNIT
SUB = 256
SCALE = math.log2(math.e) / math.sqrt(HD)
NT = (((1,), (1,)), ((), ()))
NN = (((1,), (0,)), ((), ()))
MIB = 2**20
VMEM = 58 * MIB


def groups_of(rows):
    half = rows // 2
    size = min(half, HD)
    return [
        (core * half + at, min(size, half - at)) for core in range(2) for at in range(0, half, size)
    ]


def stat_rows(rows):
    return (3 * len(groups_of(rows)) + 15) // 16 * 16


def eye_of(size):
    return lax.broadcasted_iota(jnp.int32, (size, HD), 0) == (
        lax.broadcasted_iota(jnp.int32, (size, HD), 1)
    )


def round_up(size):
    return (size + STEP - 1) // STEP * STEP


def pack(spans, own, got, out, fill):
    here = own.shape[0] // SPAN
    rows = lax.broadcasted_iota(jnp.int32, (STEP, HD), 0)
    at = jnp.int32(0)
    for passage in range(2 * here):
        source = own if passage < here else got
        base = passage % here * SPAN
        size = spans[passage]
        out[pl.ds(pl.multiple_of(at, STEP), SPAN), :] = source[base : base + SPAN, :]
        edge = jnp.minimum(size // STEP * STEP, SPAN - STEP)
        last = source[pl.ds(pl.multiple_of(base + edge, STEP), STEP), :].astype(jnp.float32)
        if fill:
            filler = jnp.broadcast_to(
                source[base : base + STEP, :].astype(jnp.float32)[:1, :], (STEP, HD)
            )
        else:
            filler = jnp.zeros((STEP, HD), jnp.float32)
        out[pl.ds(pl.multiple_of(at + edge, STEP), STEP), :] = jnp.where(
            rows + edge < size, last, filler
        ).astype(jnp.bfloat16)
        at = at + round_up(size)
    filler = filler.astype(jnp.bfloat16)
    for i in range(UNIT // STEP):
        out[pl.ds(pl.multiple_of(at + i * STEP, STEP), STEP), :] = filler


def mark(spans, passages, out):
    rows = lax.broadcasted_iota(jnp.int32, (STEP, HD), 0)
    at = jnp.int32(0)
    for passage in range(passages):
        size = spans[passage]
        out[pl.ds(pl.multiple_of(at, STEP), SPAN), :] = jnp.ones((SPAN, HD), jnp.bfloat16)
        edge = jnp.minimum(size // STEP * STEP, SPAN - STEP)
        out[pl.ds(pl.multiple_of(at + edge, STEP), STEP), :] = jnp.where(
            rows + edge < size, 1.0, 0.0
        ).astype(jnp.bfloat16)
        at = at + round_up(size)
    out[pl.ds(pl.multiple_of(at, STEP), UNIT), :] = jnp.zeros((UNIT, HD), jnp.bfloat16)


def attend_kernel(blocks, tiles, first, afters, spans, meta, *refs):
    refs = list(refs)
    take = lambda n: [refs.pop(0) for _ in range(n)]
    q_refs = take(blocks)
    if first:
        own_k, got_k, own_v, got_v = take(4)
    else:
        k_ref, v_ref = take(2)
    take(afters)
    o_refs = take(blocks)
    if first:
        k_ref, v_ref = take(2)
    q_all, m_ref, s_even, s_odd, top_even, top_odd, acc = refs
    rows = q_refs[0].shape[0]
    step = pl.program_id(0)
    passages = (k_ref.shape[0] - UNIT) // SPAN
    count = sum(round_up(spans[i]) for i in range(passages))
    units = (count + UNIT - 1) // UNIT
    turns = units // (BLOCK // UNIT)
    rest = units - turns * (BLOCK // UNIT)
    total = blocks * rows
    sub = min(SUB, total)

    def score(at, scores, top, part):
        s = lax.dot_general(
            q_all[part, :], k_ref[at, :], NT, preferred_element_type=jnp.float32
        )
        scores[part, at] = s
        most = top[part, :]
        for i in range(s.shape[1] // HD):
            most = jnp.maximum(most, s[:, i * HD : (i + 1) * HD])
        top[part, :] = most

    def weigh(at, scores, top, part):
        value = jnp.concatenate([v_ref[at, :], m_ref[at, :]], axis=1)
        most = top[part, :]
        s = scores[part, at]
        weights = jnp.concatenate(
            [
                jnp.exp2((s[:, i * HD : (i + 1) * HD] - most) * SCALE).astype(jnp.bfloat16)
                for i in range(s.shape[1] // HD)
            ],
            axis=1,
        )
        acc[part, :] += lax.dot_general(
            weights, value, NN, preferred_element_type=jnp.float32
        )

    def run(now, then):
        if then is not None:
            scores_then, top_then = then
            if first:
                pack(spans, own_v, got_v, v_ref, False)
            top_then[...] = jnp.broadcast_to(
                jnp.max(top_then[...], axis=1, keepdims=True), top_then.shape
            )
            acc[...] = jnp.zeros_like(acc)
        if now is not None:
            scores_now, top_now = now
            if first:
                pack(spans, own_k, got_k, k_ref, True)
            top_now[...] = jnp.full(top_now.shape, -3e38, jnp.float32)
            for b in range(blocks):
                q_all[b * rows : (b + 1) * rows, :] = q_refs[b][...]

        def body(start, size):
            at = pl.ds(pl.multiple_of(start, UNIT), size)
            for r in range(total // sub):
                part = pl.ds(r * sub, sub)
                if now is not None:
                    score(at, scores_now, top_now, part)
                if then is not None:
                    weigh(at, scores_then, top_then, part)

        @pl.loop(0, turns)
        def _(turn):
            body(turn * BLOCK, BLOCK)

        @pl.loop(0, rest)
        def _(turn):
            body(turns * BLOCK + turn * UNIT, UNIT)

        if then is not None:
            for b in range(blocks):
                finish(b, top_then)

    def finish(b, top):
        index = lax.broadcasted_iota(jnp.int32, (stat_rows(rows), HD), 0)
        packed = jnp.zeros(index.shape, jnp.float32)
        for u, (start, size) in enumerate(groups_of(rows)):
            part = pl.ds(b * rows + start, size)
            sums = acc[part, HD:]
            o_refs[b][start : start + size, :] = (acc[part, :HD] / sums).astype(jnp.bfloat16)
            logs = top[part, :] * SCALE + jnp.log2(sums)
            line = jnp.sum(jnp.where(eye_of(size), logs, 0.0), axis=0, keepdims=True)
            high = line.astype(jnp.bfloat16).astype(jnp.float32)
            middle = (line - high).astype(jnp.bfloat16).astype(jnp.float32)
            for i, term in enumerate((high, middle, line - high - middle)):
                packed = jnp.where(index == 3 * u + i, term, packed)
        o_refs[b][rows:, :] = packed.astype(jnp.bfloat16)

    even, odd = (s_even, top_even), (s_odd, top_odd)
    is_even = lax.rem(step, 2) == 0
    inside = jnp.logical_and(step > 0, step < tiles)

    @pl.when(step == 0)
    def _():
        mark(spans, passages, m_ref)
        run(even, None)

    if tiles > 1:

        @pl.when(jnp.logical_and(inside, is_even))
        def _():
            run(even, odd)

        @pl.when(jnp.logical_and(inside, jnp.logical_not(is_even)))
        def _():
            run(odd, even)

    @pl.when(step == tiles)
    def _():
        run(None, odd if tiles % 2 == 0 else even)


def attend(spans, meta, queries, raw, packed, after=()):
    first = packed is None
    blocks = len(queries)
    rows, width = queries[0].shape
    heads = width // HD
    tokens = raw[1].shape[0] if first else (packed[0].shape[0] - UNIT) // 2
    size = 2 * tokens + UNIT
    tall = rows + stat_rows(rows)
    now = lambda t: jnp.minimum(t, heads - 1)
    then = lambda t: jnp.maximum(t - 1, 0)
    total = blocks * rows
    packed_specs = [
        pl.BlockSpec((size, HD), lambda t, n, m: (0, now(t))),
        pl.BlockSpec((size, HD), lambda t, n, m: (0, then(t))),
    ]
    raw_specs = [
        pl.BlockSpec((tokens, HD), lambda t, n, m: (0, m[0] * heads + now(t))),
        pl.BlockSpec((tokens, HD), lambda t, n, m: (0, now(t))),
        pl.BlockSpec((tokens, HD), lambda t, n, m: (0, m[0] * heads + then(t))),
        pl.BlockSpec((tokens, HD), lambda t, n, m: (0, then(t))),
    ]
    results = pl.pallas_call(
        functools.partial(attend_kernel, blocks, heads, first, len(after)),
        grid_spec=pltpu.PrefetchScalarGridSpec(
            num_scalar_prefetch=2,
            grid=(heads + 1,),
            in_specs=[pl.BlockSpec((rows, HD), lambda t, n, m: (0, now(t)))] * blocks
            + (raw_specs if first else packed_specs)
            + [pl.BlockSpec(memory_space=pl.ANY)] * len(after),
            out_specs=[pl.BlockSpec((tall, HD), lambda t, n, m: (0, then(t)))] * blocks
            + (packed_specs if first else []),
            scratch_shapes=[
                pltpu.VMEM((total, HD), jnp.bfloat16),
                pltpu.VMEM((size, HD), jnp.bfloat16),
                pltpu.VMEM((total, size), jnp.float32),
                pltpu.VMEM((total, size), jnp.float32),
                pltpu.VMEM((total, HD), jnp.float32),
                pltpu.VMEM((total, HD), jnp.float32),
                pltpu.VMEM((total, 2 * HD), jnp.float32),
            ],
        ),
        out_shape=[jax.ShapeDtypeStruct((tall, width), jnp.bfloat16)] * blocks
        + [jax.ShapeDtypeStruct((size, width), jnp.bfloat16)] * (2 if first else 0),
        compiler_params=pltpu.CompilerParams(vmem_limit_bytes=VMEM),
        cost_estimate=pl.CostEstimate(
            flops=4 * total * size * width, bytes_accessed=4 * size * width, transcendentals=0
        ),
        name="attend",
    )(spans, meta, *queries, *(raw if first else packed), *after)
    results = list(results)
    return results[:blocks], tuple(results[blocks:]) if first else packed


def merge_kernel(count, *refs):
    parts, (keep, give) = refs[:count], refs[-2:]
    half, width = keep.shape
    rows = 2 * half
    for u, (start, size) in enumerate(groups_of(rows)):
        eye = eye_of(size)
        out, there = (keep, start) if start < half else (give, start - half)
        for head in range(width // HD):
            cols = slice(head * HD, (head + 1) * HD)
            logs = []
            for part in parts:
                stats = part[rows:, cols].astype(jnp.float32)[3 * u : 3 * u + 3]
                logs.append(stats[0:1] + (stats[1:2] + stats[2:3]))
            most = functools.reduce(jnp.maximum, logs)
            shares = [jnp.exp2(x - most) for x in logs]
            whole = functools.reduce(jnp.add, shares)
            merged = None
            for part, share in zip(parts, shares):
                line = jnp.broadcast_to(share / whole, (size, HD))
                column = jnp.sum(jnp.where(eye, line, 0.0), axis=1, keepdims=True)
                term = part[start : start + size, cols].astype(jnp.float32) * column
                merged = term if merged is None else merged + term
            out[there : there + size, cols] = merged.astype(jnp.bfloat16)


def merge(parts, half, after=()):
    width = parts[0].shape[1]
    shape = jax.ShapeDtypeStruct((half, width), jnp.bfloat16)
    return pl.pallas_call(
        functools.partial(merge_kernel, len(parts)),
        in_specs=[pl.BlockSpec(memory_space=pltpu.VMEM)] * len(parts)
        + [pl.BlockSpec(memory_space=pl.ANY)] * len(after),
        out_specs=[pl.BlockSpec(memory_space=pltpu.VMEM)] * 2,
        out_shape=[shape, shape],
        compiler_params=pltpu.CompilerParams(vmem_limit_bytes=VMEM),
        cost_estimate=pl.CostEstimate(
            flops=0, bytes_accessed=4 * half * width * len(parts), transcendentals=0
        ),
        name="merge",
    )(*parts, *after)


def project_kernel(pieces, meta, keep, got, *refs):
    weights, outs, attended = refs[:pieces], refs[pieces:-1], refs[-1]
    step = pl.program_id(0)
    width = keep.shape[1]

    @pl.when(step == 0)
    def _():
        attended[:, pl.ds(pl.multiple_of(meta[0] * width, HD), width)] = keep[...]
        attended[:, pl.ds(pl.multiple_of((1 - meta[0]) * width, HD), width)] = got[...]

    for i in range(len(outs)):

        @pl.when(step == i)
        def _(i=i):
            deep = weights[0].shape[0]
            outs[i][...] = sum(
                lax.dot_general(
                    attended[:, p * deep : (p + 1) * deep],
                    weight[...],
                    NN,
                    preferred_element_type=jnp.float32,
                )
                for p, weight in enumerate(weights)
            ).astype(outs[i].dtype)


def project(meta, keep, got, out_weight, groups):
    depth, total = out_weight.shape
    rows, width = keep.shape
    cols = total // groups
    whole = pl.BlockSpec((rows, width), lambda t, m: (0, 0))
    pieces = depth // UNIT
    return pl.pallas_call(
        functools.partial(project_kernel, pieces),
        grid_spec=pltpu.PrefetchScalarGridSpec(
            num_scalar_prefetch=1,
            grid=(groups,),
            in_specs=[whole, whole]
            + [
                pl.BlockSpec((UNIT, cols), lambda t, m, p=p: (p, m[1] ^ (groups - 1 - t)))
                for p in range(pieces)
            ],
            out_specs=[pl.BlockSpec((rows, cols), lambda t, m: (0, 0))] * groups,
            scratch_shapes=[pltpu.VMEM((rows, depth), jnp.bfloat16)],
        ),
        out_shape=[
            jax.ShapeDtypeStruct((rows, cols), jnp.bfloat16 if t < groups - 1 else jnp.float32)
            for t in range(groups)
        ],
        compiler_params=pltpu.CompilerParams(vmem_limit_bytes=VMEM),
        cost_estimate=pl.CostEstimate(
            flops=2 * rows * depth * total, bytes_accessed=2 * depth * total, transcendentals=0
        ),
        name="project",
    )(meta, keep, got, *[out_weight] * pieces)


def on_device(queries, keys, values, lengths, out_weight):
    sources = lax.axis_size("ctx")
    groups = lax.axis_size("head")
    core = lax.rem(lax.axis_index("ctx"), 2)
    width = keys.shape[1] // 2
    meta = jnp.stack([core, lax.axis_index("head")]).astype(jnp.int32)

    def swap(x, k, axis="ctx"):
        n = sources if axis == "ctx" else groups
        return lax.ppermute(x, axis, [(i, i ^ k) for i in range(n)])

    def half(x, which):
        return lax.dynamic_slice(x, (0, which * width), (x.shape[0], width))

    def back_to_owners(blocks):
        return [swap(block, 2 * i + 2) for i, block in enumerate(blocks)]

    def finish(parts, after=()):
        keep, give = merge(parts, rows, after)
        return project(meta, keep, swap(give, 1), out_weight, groups)

    def gather(blocks):
        total = blocks[-1]
        for d in range(groups - 1, 0, -1):
            total = total + swap(blocks[groups - 1 - d], d, "head").astype(jnp.float32)
        return total

    rows = queries.shape[0] // 2
    mine = half(queries, core)
    theirs = swap(half(queries, 1 - core), 1)
    ours = [jnp.concatenate([mine[:rows], theirs[:rows]]), jnp.concatenate([mine[rows:], theirs[rows:]])]
    asked = [swap(ours[0], k) for k in range(2, sources, 2)]
    keys_then, values_then, _ = lax.optimization_barrier((keys, values, ours[0]))
    got_k = swap(half(keys_then, 1 - core), 1)
    got_v = swap(half(values_then, 1 - core), 1)
    spans = jnp.concatenate([lengths, swap(lengths, 1)])
    ours[1], _ = lax.optimization_barrier((ours[1], got_v))
    asked_then = [swap(ours[1], k) for k in range(2, sources, 2)]

    raw = (keys, got_k, values, got_v)
    partial, packed = attend(spans, meta, [ours[0]] + asked, raw, None)
    back = [partial[0]] + back_to_owners(partial[1:])
    partial_then, _ = attend(spans, meta, asked_then, raw, packed)
    back_then = back_to_owners(partial_then)
    blocks = finish(back, after=partial_then[:1])
    partial_own, _ = attend(spans, meta, ours[1:], raw, packed, after=blocks[:1])
    blocks_then = finish(partial_own + back_then)
    return jnp.concatenate([gather(blocks), gather(blocks_then)], axis=0)


def solution(mesh):
    in_specs = (P("ctx", "head"), P("ctx", "head"), P("ctx", "head"), P("ctx"), P("head", None))
    out_specs = P("ctx", "head")
    return jax.shard_map(
        on_device, mesh=mesh, in_specs=in_specs, out_specs=out_specs, check_vma=False
    )
```

```python
import functools
import math

import jax
import jax.numpy as jnp
from jax import lax
from jax.experimental import pallas as pl
from jax.experimental.pallas import tpu as pltpu
from jax.sharding import PartitionSpec as P

HD = 128
SPAN = 256
STEP = 16
UNIT = 256
BLOCKS = (8 * UNIT, 2 * UNIT, UNIT)
SUB = 256
FIRST = 8
SCALE = math.log2(math.e) / math.sqrt(HD)
NT = (((1,), (1,)), ((), ()))
NN = (((1,), (0,)), ((), ()))
MIB = 2**20
VMEM = 46 * MIB
MERGE_VMEM = 12 * MIB
PROJECT_VMEM = 16 * MIB


def groups_of(rows):
    half = rows // 2
    size = min(half, HD)
    return [
        (core * half + at, min(size, half - at)) for core in range(2) for at in range(0, half, size)
    ]


def stat_rows(rows):
    return (3 * len(groups_of(rows)) + 15) // 16 * 16


def block_rows(tall):
    return next(rows for rows in range(32, tall, 32) if rows + stat_rows(rows) == tall)


def eye_of(size):
    return lax.broadcasted_iota(jnp.int32, (size, HD), 0) == (
        lax.broadcasted_iota(jnp.int32, (size, HD), 1)
    )


def round_up(size):
    return (size + STEP - 1) // STEP * STEP


def pack(spans, own, got, out, fill):
    here = own.shape[0] // SPAN
    rows = lax.broadcasted_iota(jnp.int32, (STEP, HD), 0)
    at = jnp.int32(0)
    for passage in range(2 * here):
        source = own if passage < here else got
        base = passage % here * SPAN
        size = spans[passage]
        out[pl.ds(pl.multiple_of(at, STEP), SPAN), :] = source[base : base + SPAN, :]
        edge = jnp.minimum(size // STEP * STEP, SPAN - STEP)
        last = source[pl.ds(pl.multiple_of(base + edge, STEP), STEP), :].astype(jnp.float32)
        if fill:
            filler = jnp.broadcast_to(
                source[base : base + STEP, :].astype(jnp.float32)[:1, :], (STEP, HD)
            )
        else:
            filler = jnp.zeros((STEP, HD), jnp.float32)
        out[pl.ds(pl.multiple_of(at + edge, STEP), STEP), :] = jnp.where(
            rows + edge < size, last, filler
        ).astype(jnp.bfloat16)
        at = at + round_up(size)
    filler = filler.astype(jnp.bfloat16)
    for i in range(UNIT // STEP):
        out[pl.ds(pl.multiple_of(at + i * STEP, STEP), STEP), :] = filler


def mark(spans, passages, out):
    rows = lax.broadcasted_iota(jnp.int32, (STEP, HD), 0)
    at = jnp.int32(0)
    for passage in range(passages):
        size = spans[passage]
        out[pl.ds(pl.multiple_of(at, STEP), SPAN), :] = jnp.ones((SPAN, HD), jnp.bfloat16)
        edge = jnp.minimum(size // STEP * STEP, SPAN - STEP)
        out[pl.ds(pl.multiple_of(at + edge, STEP), STEP), :] = jnp.where(
            rows + edge < size, 1.0, 0.0
        ).astype(jnp.bfloat16)
        at = at + round_up(size)
    out[pl.ds(pl.multiple_of(at, STEP), UNIT), :] = jnp.zeros((UNIT, HD), jnp.bfloat16)


def attend_kernel(blocks, tiles, first, afters, spans, meta, *refs):
    refs = list(refs)
    take = lambda n: [refs.pop(0) for _ in range(n)]
    q_refs = take(blocks)
    if first:
        own_k, got_k, own_v, got_v = take(4)
    else:
        k_ref, v_ref = take(2)
    take(afters)
    o_refs = take(blocks)
    if first:
        k_ref, v_ref = take(2)
    q_all, m_ref, s_even, s_odd, top_even, top_odd, acc = refs
    starts, total = [], 0
    for q_ref in q_refs:
        starts.append(total)
        total += q_ref.shape[0]
    step = pl.program_id(0)
    passages = (k_ref.shape[0] - UNIT) // SPAN
    count = sum(round_up(spans[i]) for i in range(passages))
    count = (count + UNIT - 1) // UNIT * UNIT
    parts = [pl.ds(r, min(SUB, total - r)) for r in range(0, total, SUB)]

    def score(at, scores, top, part):
        s = lax.dot_general(
            q_all[part, :], k_ref[at, :], NT, preferred_element_type=jnp.float32
        )
        scores[part, at] = s
        most = top[part, :]
        for i in range(s.shape[1] // HD):
            most = jnp.maximum(most, s[:, i * HD : (i + 1) * HD])
        top[part, :] = most

    def weigh(at, scores, top, part):
        value = jnp.concatenate([v_ref[at, :], m_ref[at, :]], axis=1)
        most = top[part, :]
        s = scores[part, at]
        weights = jnp.concatenate(
            [
                jnp.exp2((s[:, i * HD : (i + 1) * HD] - most) * SCALE).astype(jnp.bfloat16)
                for i in range(s.shape[1] // HD)
            ],
            axis=1,
        )
        acc[part, :] += lax.dot_general(
            weights, value, NN, preferred_element_type=jnp.float32
        )

    def run(now, then):
        if then is not None:
            scores_then, top_then = then
            if first:
                pack(spans, own_v, got_v, v_ref, False)
            top_then[...] = jnp.broadcast_to(
                jnp.max(top_then[...], axis=1, keepdims=True), top_then.shape
            )
            acc[...] = jnp.zeros_like(acc)
        if now is not None:
            scores_now, top_now = now
            if first:
                pack(spans, own_k, got_k, k_ref, True)
            top_now[...] = jnp.full(top_now.shape, -3e38, jnp.float32)
            for start, q_ref in zip(starts, q_refs):
                q_all[start : start + q_ref.shape[0], :] = q_ref[...]

        def body(start, size):
            at = pl.ds(pl.multiple_of(start, UNIT), size)
            for part in parts:
                if now is not None:
                    score(at, scores_now, top_now, part)
                if then is not None:
                    weigh(at, scores_then, top_then, part)

        start = jnp.int32(0)
        for size in BLOCKS:
            turns = (count - start) // size

            @pl.loop(0, turns)
            def _(turn, start=start, size=size):
                body(start + turn * size, size)

            start = start + turns * size

        if then is not None:
            for b in range(blocks):
                finish(b, top_then)

    def finish(b, top):
        rows = q_refs[b].shape[0]
        index = lax.broadcasted_iota(jnp.int32, (stat_rows(rows), HD), 0)
        packed = jnp.zeros(index.shape, jnp.float32)
        for u, (start, size) in enumerate(groups_of(rows)):
            part = pl.ds(starts[b] + start, size)
            sums = acc[part, HD:]
            o_refs[b][start : start + size, :] = (acc[part, :HD] / sums).astype(jnp.bfloat16)
            logs = top[part, :] * SCALE + jnp.log2(sums)
            line = jnp.sum(jnp.where(eye_of(size), logs, 0.0), axis=0, keepdims=True)
            high = line.astype(jnp.bfloat16).astype(jnp.float32)
            middle = (line - high).astype(jnp.bfloat16).astype(jnp.float32)
            for i, term in enumerate((high, middle, line - high - middle)):
                packed = jnp.where(index == 3 * u + i, term, packed)
        o_refs[b][rows:, :] = packed.astype(jnp.bfloat16)

    even, odd = (s_even, top_even), (s_odd, top_odd)
    is_even = lax.rem(step, 2) == 0
    inside = jnp.logical_and(step > 0, step < tiles)

    @pl.when(step == 0)
    def _():
        mark(spans, passages, m_ref)
        run(even, None)

    if tiles > 1:

        @pl.when(jnp.logical_and(inside, is_even))
        def _():
            run(even, odd)

        @pl.when(jnp.logical_and(inside, jnp.logical_not(is_even)))
        def _():
            run(odd, even)

    @pl.when(step == tiles)
    def _():
        run(None, odd if tiles % 2 == 0 else even)


def attend(spans, meta, queries, raw, packed, after=()):
    first = packed is None
    blocks = len(queries)
    heights = [x.shape[0] for x in queries]
    tall = [rows + stat_rows(rows) for rows in heights]
    total = sum(heights)
    width = queries[0].shape[1]
    heads = width // HD
    tokens = raw[1].shape[0] if first else (packed[0].shape[1] - UNIT) // 2
    size = 2 * tokens + UNIT
    now = lambda t: jnp.minimum(t, heads - 1)
    then = lambda t: jnp.maximum(t - 1, 0)
    packed_specs = [
        pl.BlockSpec((None, size, HD), lambda t, n, m: (now(t), 0, 0)),
        pl.BlockSpec((None, size, HD), lambda t, n, m: (then(t), 0, 0)),
    ]
    raw_specs = [
        pl.BlockSpec((tokens, HD), lambda t, n, m: (0, m[0] * heads + now(t))),
        pl.BlockSpec((tokens, HD), lambda t, n, m: (0, now(t))),
        pl.BlockSpec((tokens, HD), lambda t, n, m: (0, m[0] * heads + then(t))),
        pl.BlockSpec((tokens, HD), lambda t, n, m: (0, then(t))),
    ]
    results = pl.pallas_call(
        functools.partial(attend_kernel, blocks, heads, first, len(after)),
        grid_spec=pltpu.PrefetchScalarGridSpec(
            num_scalar_prefetch=2,
            grid=(heads + 1,),
            in_specs=[pl.BlockSpec((rows, HD), lambda t, n, m: (0, now(t))) for rows in heights]
            + (raw_specs if first else packed_specs)
            + [pl.BlockSpec(memory_space=pl.ANY)] * len(after),
            out_specs=[pl.BlockSpec((rows, HD), lambda t, n, m: (0, then(t))) for rows in tall]
            + (packed_specs if first else []),
            scratch_shapes=[
                pltpu.VMEM((total, HD), jnp.bfloat16),
                pltpu.VMEM((size, HD), jnp.bfloat16),
                pltpu.VMEM((total, size), jnp.float32),
                pltpu.VMEM((total, size), jnp.float32),
                pltpu.VMEM((total, HD), jnp.float32),
                pltpu.VMEM((total, HD), jnp.float32),
                pltpu.VMEM((total, 2 * HD), jnp.float32),
            ],
        ),
        out_shape=[jax.ShapeDtypeStruct((rows, width), jnp.bfloat16) for rows in tall]
        + [jax.ShapeDtypeStruct((heads, size, HD), jnp.bfloat16)] * (2 if first else 0),
        compiler_params=pltpu.CompilerParams(vmem_limit_bytes=VMEM),
        cost_estimate=pl.CostEstimate(
            flops=4 * total * size * width, bytes_accessed=4 * size * width, transcendentals=0
        ),
        name="attend",
    )(spans, meta, *queries, *(raw if first else packed), *after)
    results = list(results)
    return results[:blocks], tuple(results[blocks:]) if first else packed


def merge_kernel(count, *refs):
    parts, (keep, give) = refs[:count], refs[-2:]
    half, width = keep.shape
    rows = 2 * half
    for u, (start, size) in enumerate(groups_of(rows)):
        eye = eye_of(size)
        out, there = (keep, start) if start < half else (give, start - half)
        for head in range(width // HD):
            cols = slice(head * HD, (head + 1) * HD)
            logs = []
            for part in parts:
                stats = part[rows:, cols].astype(jnp.float32)[3 * u : 3 * u + 3]
                logs.append(stats[0:1] + (stats[1:2] + stats[2:3]))
            most = functools.reduce(jnp.maximum, logs)
            shares = [jnp.exp2(x - most) for x in logs]
            whole = functools.reduce(jnp.add, shares)
            merged = None
            for part, share in zip(parts, shares):
                line = jnp.broadcast_to(share / whole, (size, HD))
                column = jnp.sum(jnp.where(eye, line, 0.0), axis=1, keepdims=True)
                term = part[start : start + size, cols].astype(jnp.float32) * column
                merged = term if merged is None else merged + term
            out[there : there + size, cols] = merged.astype(jnp.bfloat16)


def merge(parts, after=()):
    width = parts[0].shape[1]
    half = block_rows(parts[0].shape[0]) // 2
    shape = jax.ShapeDtypeStruct((half, width), jnp.bfloat16)
    return pl.pallas_call(
        functools.partial(merge_kernel, len(parts)),
        in_specs=[pl.BlockSpec(memory_space=pltpu.VMEM)] * len(parts)
        + [pl.BlockSpec(memory_space=pl.ANY)] * len(after),
        out_specs=[pl.BlockSpec(memory_space=pltpu.VMEM)] * 2,
        out_shape=[shape, shape],
        compiler_params=pltpu.CompilerParams(vmem_limit_bytes=MERGE_VMEM),
        cost_estimate=pl.CostEstimate(
            flops=0, bytes_accessed=4 * half * width * len(parts), transcendentals=0
        ),
        name="merge",
    )(*parts, *after)


def project_kernel(meta, keep, got, weight, *refs):
    groups = (len(refs) - 2) // 2
    outs, made, attended, done = refs[:groups], refs[groups : 2 * groups], refs[-2], refs[-1]
    width = keep.shape[1]
    cols = outs[0].shape[1]
    attended[:, pl.ds(pl.multiple_of(meta[0] * width, HD), width)] = keep[...]
    attended[:, pl.ds(pl.multiple_of((1 - meta[0]) * width, HD), width)] = got[...]
    order = list(reversed(range(groups)))
    copies = [pltpu.make_async_copy(made[d], outs[d], done.at[d]) for d in range(groups)]
    for d in order:
        at = pl.ds(pl.multiple_of((meta[1] ^ d) * cols, HD), cols)
        made[d][...] = lax.dot_general(
            attended[...], weight[:, at], NN, preferred_element_type=jnp.float32
        ).astype(made[d].dtype)
        copies[d].start()
    for d in order:
        copies[d].wait()


def project(meta, keep, got, out_weight, groups):
    depth, total = out_weight.shape
    rows, width = keep.shape
    cols = total // groups
    types = [jnp.float32] + [jnp.bfloat16] * (groups - 1)
    return pl.pallas_call(
        project_kernel,
        in_specs=[pl.BlockSpec(memory_space=pltpu.SMEM)]
        + [pl.BlockSpec(memory_space=pltpu.VMEM)] * 3,
        out_specs=[pl.BlockSpec(memory_space=pl.ANY)] * groups,
        scratch_shapes=[pltpu.VMEM((rows, cols), kind) for kind in types]
        + [pltpu.VMEM((rows, depth), jnp.bfloat16), pltpu.SemaphoreType.DMA((groups,))],
        out_shape=[jax.ShapeDtypeStruct((rows, cols), kind) for kind in types],
        compiler_params=pltpu.CompilerParams(vmem_limit_bytes=PROJECT_VMEM),
        cost_estimate=pl.CostEstimate(
            flops=2 * rows * depth * total, bytes_accessed=2 * depth * total, transcendentals=0
        ),
        name="project",
    )(meta, keep, got, out_weight)


def total_kernel(count, *refs):
    out = refs[-1]
    out[...] = refs[0][...] + sum(ref[...].astype(jnp.float32) for ref in refs[1:count])


def add_up(parts, start, total, before):
    rows, cols = parts[0].shape
    step = math.gcd(math.gcd(rows, start), 32)
    return pl.pallas_call(
        functools.partial(total_kernel, len(parts)),
        grid=(rows // step,),
        in_specs=[pl.BlockSpec((step, cols), lambda t: (t, 0))] * len(parts)
        + [pl.BlockSpec(memory_space=pl.ANY)] * len(before),
        out_specs=pl.BlockSpec((step, cols), lambda t: (start // step + t, 0)),
        out_shape=jax.ShapeDtypeStruct((total, cols), jnp.float32),
        input_output_aliases={len(parts): 0} if before else {},
        compiler_params=pltpu.CompilerParams(vmem_limit_bytes=MERGE_VMEM),
        cost_estimate=pl.CostEstimate(
            flops=0, bytes_accessed=2 * rows * cols * (len(parts) + 3), transcendentals=0
        ),
        name="add_up",
    )(*parts, *before)


def first_rows(rows):
    return (rows * FIRST // 16 + STEP - 1) // STEP * STEP


def on_device(queries, keys, values, lengths, out_weight):
    sources = lax.axis_size("ctx")
    groups = lax.axis_size("head")
    core = lax.rem(lax.axis_index("ctx"), 2)
    width = keys.shape[1] // 2
    meta = jnp.stack([core, lax.axis_index("head")]).astype(jnp.int32)

    def swap(x, k, axis="ctx"):
        n = sources if axis == "ctx" else groups
        return lax.ppermute(x, axis, [(i, i ^ k) for i in range(n)])

    def half(x, which):
        return lax.dynamic_slice(x, (0, which * width), (x.shape[0], width))

    def others_of(x):
        return [swap(x, k) for k in reversed(range(2, sources, 2))]

    def back_to_owners(blocks):
        return [swap(block, k) for block, k in zip(blocks, reversed(range(2, sources, 2)))]

    def finish(parts, after=()):
        keep, give = merge(parts, after)
        return project(meta, keep, swap(give, 1), out_weight, groups)

    def arrive(blocks):
        far = [swap(blocks[d], d, "head") for d in reversed(range(1, groups))]
        return [blocks[0]] + far

    rows = first_rows(queries.shape[0])
    mine = half(queries, core)
    theirs = swap(half(queries, 1 - core), 1)
    keys_then, values_then, _ = lax.optimization_barrier((keys, values, theirs))
    got_k = swap(half(keys_then, 1 - core), 1)
    got_v = swap(half(values_then, 1 - core), 1)
    ours = [jnp.concatenate([mine[:rows], theirs[:rows]]), jnp.concatenate([mine[rows:], theirs[rows:]])]
    asked = others_of(ours[0])
    spans = jnp.concatenate([lengths, swap(lengths, 1)])
    late, _ = lax.optimization_barrier((ours[1], got_v))
    asked_then = others_of(late)

    raw = (keys, got_k, values, got_v)
    own, packed = attend(spans, meta, ours, raw, None)
    partial, _ = attend(spans, meta, asked, raw, packed)
    back = back_to_owners(partial)
    partial_then, _ = attend(spans, meta, asked_then, raw, packed, after=partial[:1])
    back_then = back_to_owners(partial_then)
    blocks = finish(own[:1] + back, after=partial_then[:1])
    blocks_then = finish(own[1:] + back_then, after=blocks[:1])
    out = add_up(arrive(blocks), 0, queries.shape[0], ())
    return add_up(arrive(blocks_then), rows, queries.shape[0], (out,))


def solution(mesh):
    in_specs = (P("ctx", "head"), P("ctx", "head"), P("ctx", "head"), P("ctx"), P("head", None))
    out_specs = P("ctx", "head")
    return jax.shard_map(
        on_device, mesh=mesh, in_specs=in_specs, out_specs=out_specs, check_vma=False
    )
```

```python
import functools
import math

import jax
import jax.numpy as jnp
from jax import lax
from jax.experimental import pallas as pl
from jax.experimental.pallas import tpu as pltpu
from jax.sharding import PartitionSpec as P

HD = 128
SPAN = 256
STEP = 16
UNIT = 256
BLOCKS = (8 * UNIT, 2 * UNIT, UNIT)
SUB = 256
PARTS = (2, 1, 1)
SCALE = math.log2(math.e) / math.sqrt(HD)
NT = (((1,), (1,)), ((), ()))
NN = (((1,), (0,)), ((), ()))
MIB = 2**20
VMEM = 53 * MIB
MERGE_VMEM = 12 * MIB
PROJECT_VMEM = 16 * MIB


def groups_of(rows):
    half = rows // 2
    size = min(half, HD)
    return [
        (core * half + at, min(size, half - at)) for core in range(2) for at in range(0, half, size)
    ]


def stat_rows(rows):
    return (3 * len(groups_of(rows)) + 15) // 16 * 16


def block_rows(tall):
    return next(rows for rows in range(32, tall, 32) if rows + stat_rows(rows) == tall)


def eye_of(size):
    return lax.broadcasted_iota(jnp.int32, (size, HD), 0) == (
        lax.broadcasted_iota(jnp.int32, (size, HD), 1)
    )


def round_up(size):
    return (size + STEP - 1) // STEP * STEP


def pack(spans, own, got, out, fill):
    here = own.shape[0] // SPAN
    rows = lax.broadcasted_iota(jnp.int32, (STEP, HD), 0)
    at = jnp.int32(0)
    for passage in range(2 * here):
        source = own if passage < here else got
        base = passage % here * SPAN
        size = spans[passage]
        out[pl.ds(pl.multiple_of(at, STEP), SPAN), :] = source[base : base + SPAN, :]
        edge = jnp.minimum(size // STEP * STEP, SPAN - STEP)
        last = source[pl.ds(pl.multiple_of(base + edge, STEP), STEP), :].astype(jnp.float32)
        if fill:
            filler = jnp.broadcast_to(
                source[base : base + STEP, :].astype(jnp.float32)[:1, :], (STEP, HD)
            )
        else:
            filler = jnp.zeros((STEP, HD), jnp.float32)
        out[pl.ds(pl.multiple_of(at + edge, STEP), STEP), :] = jnp.where(
            rows + edge < size, last, filler
        ).astype(jnp.bfloat16)
        at = at + round_up(size)
    filler = filler.astype(jnp.bfloat16)
    for i in range(UNIT // STEP):
        out[pl.ds(pl.multiple_of(at + i * STEP, STEP), STEP), :] = filler


def mark(spans, passages, out):
    rows = lax.broadcasted_iota(jnp.int32, (STEP, HD), 0)
    at = jnp.int32(0)
    for passage in range(passages):
        size = spans[passage]
        out[pl.ds(pl.multiple_of(at, STEP), SPAN), :] = jnp.ones((SPAN, HD), jnp.bfloat16)
        edge = jnp.minimum(size // STEP * STEP, SPAN - STEP)
        out[pl.ds(pl.multiple_of(at + edge, STEP), STEP), :] = jnp.where(
            rows + edge < size, 1.0, 0.0
        ).astype(jnp.bfloat16)
        at = at + round_up(size)
    out[pl.ds(pl.multiple_of(at, STEP), UNIT), :] = jnp.zeros((UNIT, HD), jnp.bfloat16)


def attend_kernel(blocks, tiles, first, afters, spans, meta, *refs):
    refs = list(refs)
    take = lambda n: [refs.pop(0) for _ in range(n)]
    q_refs = take(blocks)
    if first:
        own_k, got_k, own_v, got_v = take(4)
    else:
        k_ref, v_ref = take(2)
    take(afters)
    o_refs = take(blocks)
    if first:
        k_ref, v_ref = take(2)
    q_all, m_ref, s_even, s_odd, top_even, top_odd, acc = refs
    starts, total = [], 0
    for q_ref in q_refs:
        starts.append(total)
        total += q_ref.shape[0]
    step = pl.program_id(0)
    passages = (k_ref.shape[0] - UNIT) // SPAN
    count = sum(round_up(spans[i]) for i in range(passages))
    count = (count + UNIT - 1) // UNIT * UNIT
    parts = [pl.ds(r, min(SUB, total - r)) for r in range(0, total, SUB)]

    def score(at, scores, top, part):
        s = lax.dot_general(
            q_all[part, :], k_ref[at, :], NT, preferred_element_type=jnp.float32
        )
        scores[part, at] = s
        most = top[part, :]
        for i in range(s.shape[1] // HD):
            most = jnp.maximum(most, s[:, i * HD : (i + 1) * HD])
        top[part, :] = most

    def weigh(at, scores, top, part):
        value = jnp.concatenate([v_ref[at, :], m_ref[at, :]], axis=1)
        most = top[part, :]
        s = scores[part, at]
        weights = jnp.concatenate(
            [
                jnp.exp2((s[:, i * HD : (i + 1) * HD] - most) * SCALE).astype(jnp.bfloat16)
                for i in range(s.shape[1] // HD)
            ],
            axis=1,
        )
        acc[part, :] += lax.dot_general(
            weights, value, NN, preferred_element_type=jnp.float32
        )

    def run(now, then):
        if then is not None:
            scores_then, top_then = then
            if first:
                pack(spans, own_v, got_v, v_ref, False)
            top_then[...] = jnp.broadcast_to(
                jnp.max(top_then[...], axis=1, keepdims=True), top_then.shape
            )
            acc[...] = jnp.zeros_like(acc)
        if now is not None:
            scores_now, top_now = now
            if first:
                pack(spans, own_k, got_k, k_ref, True)
            top_now[...] = jnp.full(top_now.shape, -3e38, jnp.float32)
            for start, q_ref in zip(starts, q_refs):
                q_all[start : start + q_ref.shape[0], :] = q_ref[...]

        def body(start, size):
            at = pl.ds(pl.multiple_of(start, UNIT), size)
            for part in parts:
                if now is not None:
                    score(at, scores_now, top_now, part)
                if then is not None:
                    weigh(at, scores_then, top_then, part)

        start = jnp.int32(0)
        for size in BLOCKS:
            turns = (count - start) // size

            @pl.loop(0, turns)
            def _(turn, start=start, size=size):
                body(start + turn * size, size)

            start = start + turns * size

        if then is not None:
            for b in range(blocks):
                finish(b, top_then)

    def finish(b, top):
        rows = q_refs[b].shape[0]
        index = lax.broadcasted_iota(jnp.int32, (stat_rows(rows), HD), 0)
        packed = jnp.zeros(index.shape, jnp.float32)
        for u, (start, size) in enumerate(groups_of(rows)):
            part = pl.ds(starts[b] + start, size)
            sums = acc[part, HD:]
            o_refs[b][start : start + size, :] = (acc[part, :HD] / sums).astype(jnp.bfloat16)
            logs = top[part, :] * SCALE + jnp.log2(sums)
            line = jnp.sum(jnp.where(eye_of(size), logs, 0.0), axis=0, keepdims=True)
            high = line.astype(jnp.bfloat16).astype(jnp.float32)
            middle = (line - high).astype(jnp.bfloat16).astype(jnp.float32)
            for i, term in enumerate((high, middle, line - high - middle)):
                packed = jnp.where(index == 3 * u + i, term, packed)
        o_refs[b][rows:, :] = packed.astype(jnp.bfloat16)

    even, odd = (s_even, top_even), (s_odd, top_odd)
    is_even = lax.rem(step, 2) == 0
    inside = jnp.logical_and(step > 0, step < tiles)

    @pl.when(step == 0)
    def _():
        mark(spans, passages, m_ref)
        run(even, None)

    if tiles > 1:

        @pl.when(jnp.logical_and(inside, is_even))
        def _():
            run(even, odd)

        @pl.when(jnp.logical_and(inside, jnp.logical_not(is_even)))
        def _():
            run(odd, even)

    @pl.when(step == tiles)
    def _():
        run(None, odd if tiles % 2 == 0 else even)


def attend(spans, meta, queries, raw, packed, after=()):
    first = packed is None
    blocks = len(queries)
    heights = [rows for _, _, rows in queries]
    tall = [rows + stat_rows(rows) for rows in heights]
    total = sum(heights)
    width = queries[0][0].shape[1]
    heads = width // HD
    tokens = raw[1].shape[0] if first else (packed[0].shape[1] - UNIT) // 2
    size = 2 * tokens + UNIT
    now = lambda t: jnp.minimum(t, heads - 1)
    then = lambda t: jnp.maximum(t - 1, 0)
    packed_specs = [
        pl.BlockSpec((None, size, HD), lambda t, n, m: (now(t), 0, 0)),
        pl.BlockSpec((None, size, HD), lambda t, n, m: (then(t), 0, 0)),
    ]
    raw_specs = [
        pl.BlockSpec((tokens, HD), lambda t, n, m: (0, m[0] * heads + now(t))),
        pl.BlockSpec((tokens, HD), lambda t, n, m: (0, now(t))),
        pl.BlockSpec((tokens, HD), lambda t, n, m: (0, m[0] * heads + then(t))),
        pl.BlockSpec((tokens, HD), lambda t, n, m: (0, then(t))),
    ]
    results = pl.pallas_call(
        functools.partial(attend_kernel, blocks, heads, first, len(after)),
        grid_spec=pltpu.PrefetchScalarGridSpec(
            num_scalar_prefetch=2,
            grid=(heads + 1,),
            in_specs=[
                pl.BlockSpec((rows, HD), lambda t, n, m, i=i: (i, now(t))) for _, i, rows in queries
            ]
            + (raw_specs if first else packed_specs)
            + [pl.BlockSpec(memory_space=pl.ANY)] * len(after),
            out_specs=[pl.BlockSpec((rows, HD), lambda t, n, m: (0, then(t))) for rows in tall]
            + (packed_specs if first else []),
            scratch_shapes=[
                pltpu.VMEM((total, HD), jnp.bfloat16),
                pltpu.VMEM((size, HD), jnp.bfloat16),
                pltpu.VMEM((total, size), jnp.float32),
                pltpu.VMEM((total, size), jnp.float32),
                pltpu.VMEM((total, HD), jnp.float32),
                pltpu.VMEM((total, HD), jnp.float32),
                pltpu.VMEM((total, 2 * HD), jnp.float32),
            ],
        ),
        out_shape=[jax.ShapeDtypeStruct((rows, width), jnp.bfloat16) for rows in tall]
        + [jax.ShapeDtypeStruct((heads, size, HD), jnp.bfloat16)] * (2 if first else 0),
        compiler_params=pltpu.CompilerParams(vmem_limit_bytes=VMEM),
        cost_estimate=pl.CostEstimate(
            flops=4 * total * size * width, bytes_accessed=4 * size * width, transcendentals=0
        ),
        name="attend",
    )(spans, meta, *[x for x, _, _ in queries], *(raw if first else packed), *after)
    results = list(results)
    return results[:blocks], tuple(results[blocks:]) if first else packed


def merge_kernel(count, *refs):
    parts, (keep, give) = refs[:count], refs[-2:]
    half, width = keep.shape
    rows = 2 * half
    for u, (start, size) in enumerate(groups_of(rows)):
        eye = eye_of(size)
        out, there = (keep, start) if start < half else (give, start - half)
        for head in range(width // HD):
            cols = slice(head * HD, (head + 1) * HD)
            logs = []
            for part in parts:
                stats = part[rows:, cols].astype(jnp.float32)[3 * u : 3 * u + 3]
                logs.append(stats[0:1] + (stats[1:2] + stats[2:3]))
            most = functools.reduce(jnp.maximum, logs)
            shares = [jnp.exp2(x - most) for x in logs]
            whole = functools.reduce(jnp.add, shares)
            merged = None
            for part, share in zip(parts, shares):
                line = jnp.broadcast_to(share / whole, (size, HD))
                column = jnp.sum(jnp.where(eye, line, 0.0), axis=1, keepdims=True)
                term = part[start : start + size, cols].astype(jnp.float32) * column
                merged = term if merged is None else merged + term
            out[there : there + size, cols] = merged.astype(jnp.bfloat16)


def merge(parts, after=()):
    width = parts[0].shape[1]
    half = block_rows(parts[0].shape[0]) // 2
    shape = jax.ShapeDtypeStruct((half, width), jnp.bfloat16)
    return pl.pallas_call(
        functools.partial(merge_kernel, len(parts)),
        in_specs=[pl.BlockSpec(memory_space=pltpu.VMEM)] * len(parts)
        + [pl.BlockSpec(memory_space=pl.ANY)] * len(after),
        out_specs=[pl.BlockSpec(memory_space=pltpu.VMEM)] * 2,
        out_shape=[shape, shape],
        compiler_params=pltpu.CompilerParams(vmem_limit_bytes=MERGE_VMEM),
        cost_estimate=pl.CostEstimate(
            flops=0, bytes_accessed=4 * half * width * len(parts), transcendentals=0
        ),
        name="merge",
    )(*parts, *after)


def project_kernel(meta, keep, got, weight, *refs):
    groups = (len(refs) - 2) // 2
    outs, made, attended, done = refs[:groups], refs[groups : 2 * groups], refs[-2], refs[-1]
    width = keep.shape[1]
    cols = outs[0].shape[1]
    attended[:, pl.ds(pl.multiple_of(meta[0] * width, HD), width)] = keep[...]
    attended[:, pl.ds(pl.multiple_of((1 - meta[0]) * width, HD), width)] = got[...]
    order = list(reversed(range(groups)))
    copies = [pltpu.make_async_copy(made[d], outs[d], done.at[d]) for d in range(groups)]
    for d in order:
        at = pl.ds(pl.multiple_of((meta[1] ^ d) * cols, HD), cols)
        made[d][...] = lax.dot_general(
            attended[...], weight[:, at], NN, preferred_element_type=jnp.float32
        ).astype(made[d].dtype)
        copies[d].start()
    for d in order:
        copies[d].wait()


def project(meta, keep, got, out_weight, groups):
    depth, total = out_weight.shape
    rows, width = keep.shape
    cols = total // groups
    types = [jnp.float32] + [jnp.bfloat16] * (groups - 1)
    return pl.pallas_call(
        project_kernel,
        in_specs=[pl.BlockSpec(memory_space=pltpu.SMEM)]
        + [pl.BlockSpec(memory_space=pltpu.VMEM)] * 3,
        out_specs=[pl.BlockSpec(memory_space=pl.ANY)] * groups,
        scratch_shapes=[pltpu.VMEM((rows, cols), kind) for kind in types]
        + [pltpu.VMEM((rows, depth), jnp.bfloat16), pltpu.SemaphoreType.DMA((groups,))],
        out_shape=[jax.ShapeDtypeStruct((rows, cols), kind) for kind in types],
        compiler_params=pltpu.CompilerParams(vmem_limit_bytes=PROJECT_VMEM),
        cost_estimate=pl.CostEstimate(
            flops=2 * rows * depth * total, bytes_accessed=2 * depth * total, transcendentals=0
        ),
        name="project",
    )(meta, keep, got, out_weight)


def total_kernel(count, *refs):
    out = refs[-1]
    out[...] = refs[0][...] + sum(ref[...].astype(jnp.float32) for ref in refs[1:count])


def add_up(parts, start, total, before):
    rows, cols = parts[0].shape
    step = math.gcd(math.gcd(rows, start), 32)
    return pl.pallas_call(
        functools.partial(total_kernel, len(parts)),
        grid=(rows // step,),
        in_specs=[pl.BlockSpec((step, cols), lambda t: (t, 0))] * len(parts)
        + [pl.BlockSpec(memory_space=pl.ANY)] * len(before),
        out_specs=pl.BlockSpec((step, cols), lambda t: (start // step + t, 0)),
        out_shape=jax.ShapeDtypeStruct((total, cols), jnp.float32),
        input_output_aliases={len(parts): 0} if before else {},
        compiler_params=pltpu.CompilerParams(vmem_limit_bytes=MERGE_VMEM),
        cost_estimate=pl.CostEstimate(
            flops=0, bytes_accessed=2 * rows * cols * (len(parts) + 3), transcendentals=0
        ),
        name="add_up",
    )(*parts, *before)


def on_device(queries, keys, values, lengths, out_weight):
    sources = lax.axis_size("ctx")
    groups = lax.axis_size("head")
    core = lax.rem(lax.axis_index("ctx"), 2)
    width = keys.shape[1] // 2
    meta = jnp.stack([core, lax.axis_index("head")]).astype(jnp.int32)

    def swap(x, k, axis="ctx"):
        n = sources if axis == "ctx" else groups
        return lax.ppermute(x, axis, [(i, i ^ k) for i in range(n)])

    def half(x, which):
        return lax.dynamic_slice(x, (0, which * width), (x.shape[0], width))

    def others_of(x):
        return [swap(x, k) for k in reversed(range(2, sources, 2))]

    def back_to_owners(blocks):
        return [swap(block, k) for block, k in zip(blocks, reversed(range(2, sources, 2)))]

    def finish(parts, after=()):
        keep, give = merge(parts, after)
        return project(meta, keep, swap(give, 1), out_weight, groups)

    def arrive(blocks):
        far = [swap(blocks[d], d, "head") for d in reversed(range(1, groups))]
        return [blocks[0]] + far

    mine = half(queries, core)
    theirs = swap(half(queries, 1 - core), 1)
    keys_then, values_then, _ = lax.optimization_barrier((keys, values, theirs))
    got_k = swap(half(keys_then, 1 - core), 1)
    got_v = swap(half(values_then, 1 - core), 1)
    cuts = [0]
    for part in PARTS:
        cuts.append(cuts[-1] + queries.shape[0] * part // sum(PARTS))
    pairs = [x[cuts[i] : cuts[i + 1]] for i in range(3) for x in (mine, theirs)]
    early, late = jnp.concatenate(pairs[:2]), jnp.concatenate(pairs[2:])
    rows = [2 * (cuts[i + 1] - cuts[i]) for i in range(3)]
    asked = others_of(early)
    spans = jnp.concatenate([lengths, swap(lengths, 1)])
    late, _ = lax.optimization_barrier((late, got_v))
    asked_late = others_of(late)

    raw = (keys, got_k, values, got_v)
    own, packed = attend(
        spans, meta, [(early, 0, rows[0]), (late, 0, rows[1]), (late, 1, rows[2])], raw, None
    )

    def others(x, index, size, after):
        partial, _ = attend(spans, meta, [(q, index, size) for q in x], raw, packed, after)
        return partial, back_to_owners(partial)

    done, back_0 = others(asked, 0, rows[0], ())
    done, back_1 = others(asked_late, 0, rows[1], done[:1])
    blocks_0 = finish(own[:1] + back_0, done[:1])
    done, back_2 = others(asked_late, 1, rows[2], blocks_0[:1])
    blocks_1 = finish(own[1:2] + back_1, done[:1])
    there_0 = arrive(blocks_0)
    blocks_1, there_0 = lax.optimization_barrier((blocks_1, there_0))
    there_1 = arrive(blocks_1)
    blocks_2 = finish(own[2:] + back_2, blocks_1[:1])
    there_2 = arrive(blocks_2)
    total = queries.shape[0]
    out = add_up(there_0, cuts[0], total, ())
    out = add_up(there_1, cuts[1], total, (out,))
    return add_up(there_2, cuts[2], total, (out,))


def solution(mesh):
    in_specs = (P("ctx", "head"), P("ctx", "head"), P("ctx", "head"), P("ctx"), P("head", None))
    out_specs = P("ctx", "head")
    return jax.shard_map(
        on_device, mesh=mesh, in_specs=in_specs, out_specs=out_specs, check_vma=False
    )
```

```python
import functools
import math

import jax
import jax.numpy as jnp
from jax import lax
from jax.experimental import pallas as pl
from jax.experimental.pallas import tpu as pltpu
from jax.sharding import PartitionSpec as P

HD = 128
SPAN = 256
STEP = 16
UNIT = 256
BLOCKS = (8 * UNIT, 3 * UNIT, 2 * UNIT, UNIT)
SUB = 256
PARTS = (2, 1, 1)
SCALE = math.log2(math.e) / math.sqrt(HD)
NT = (((1,), (1,)), ((), ()))
NN = (((1,), (0,)), ((), ()))
MIB = 2**20
VMEM = 53 * MIB
MERGE_VMEM = 12 * MIB
PROJECT_VMEM = 16 * MIB


def groups_of(rows):
    half = rows // 2
    size = min(half, HD)
    return [
        (core * half + at, min(size, half - at)) for core in range(2) for at in range(0, half, size)
    ]


def stat_rows(rows):
    return (3 * len(groups_of(rows)) + 15) // 16 * 16


def block_rows(tall):
    return next(rows for rows in range(32, tall, 32) if rows + stat_rows(rows) == tall)


def eye_of(size):
    return lax.broadcasted_iota(jnp.int32, (size, HD), 0) == (
        lax.broadcasted_iota(jnp.int32, (size, HD), 1)
    )


def round_up(size):
    return (size + STEP - 1) // STEP * STEP


def pack(spans, own, got, out, fill):
    here = own.shape[0] // SPAN
    rows = lax.broadcasted_iota(jnp.int32, (STEP, HD), 0)
    at = jnp.int32(0)
    for passage in range(2 * here):
        source = own if passage < here else got
        base = passage % here * SPAN
        size = spans[passage]
        out[pl.ds(pl.multiple_of(at, STEP), SPAN), :] = source[base : base + SPAN, :]
        edge = jnp.minimum(size // STEP * STEP, SPAN - STEP)
        last = source[pl.ds(pl.multiple_of(base + edge, STEP), STEP), :].astype(jnp.float32)
        if fill:
            filler = jnp.broadcast_to(
                source[base : base + STEP, :].astype(jnp.float32)[:1, :], (STEP, HD)
            )
        else:
            filler = jnp.zeros((STEP, HD), jnp.float32)
        out[pl.ds(pl.multiple_of(at + edge, STEP), STEP), :] = jnp.where(
            rows + edge < size, last, filler
        ).astype(jnp.bfloat16)
        at = at + round_up(size)
    filler = filler.astype(jnp.bfloat16)
    for i in range(UNIT // STEP):
        out[pl.ds(pl.multiple_of(at + i * STEP, STEP), STEP), :] = filler


def mark(spans, passages, out):
    rows = lax.broadcasted_iota(jnp.int32, (STEP, HD), 0)
    at = jnp.int32(0)
    for passage in range(passages):
        size = spans[passage]
        out[pl.ds(pl.multiple_of(at, STEP), SPAN), :] = jnp.ones((SPAN, HD), jnp.bfloat16)
        edge = jnp.minimum(size // STEP * STEP, SPAN - STEP)
        out[pl.ds(pl.multiple_of(at + edge, STEP), STEP), :] = jnp.where(
            rows + edge < size, 1.0, 0.0
        ).astype(jnp.bfloat16)
        at = at + round_up(size)
    out[pl.ds(pl.multiple_of(at, STEP), UNIT), :] = jnp.zeros((UNIT, HD), jnp.bfloat16)


def attend_kernel(blocks, tiles, first, afters, own_spans, got_spans, meta, *refs):
    here = own_spans.shape[0]
    spans = [own_spans[i] for i in range(here)] + [got_spans[i] for i in range(here)]
    refs = list(refs)
    take = lambda n: [refs.pop(0) for _ in range(n)]
    q_refs = take(blocks)
    if first:
        own_k, got_k, own_v, got_v = take(4)
    else:
        k_ref, v_ref = take(2)
    take(afters)
    o_refs = take(blocks)
    if first:
        k_ref, v_ref = take(2)
    q_all, m_ref, s_even, s_odd, top_even, top_odd, acc = refs
    starts, total = [], 0
    for q_ref in q_refs:
        starts.append(total)
        total += q_ref.shape[0]
    step = pl.program_id(0)
    passages = (k_ref.shape[0] - UNIT) // SPAN
    count = sum(round_up(spans[i]) for i in range(passages))
    count = (count + UNIT - 1) // UNIT * UNIT
    parts = [pl.ds(r, min(SUB, total - r)) for r in range(0, total, SUB)]

    def score(at, scores, top, part):
        s = lax.dot_general(
            q_all[part, :], k_ref[at, :], NT, preferred_element_type=jnp.float32
        )
        scores[part, at] = s
        most = top[part, :]
        for i in range(s.shape[1] // HD):
            most = jnp.maximum(most, s[:, i * HD : (i + 1) * HD])
        top[part, :] = most

    def weigh(at, scores, top, part):
        value = jnp.concatenate([v_ref[at, :], m_ref[at, :]], axis=1)
        most = top[part, :]
        s = scores[part, at]
        weights = jnp.concatenate(
            [
                jnp.exp2((s[:, i * HD : (i + 1) * HD] - most) * SCALE).astype(jnp.bfloat16)
                for i in range(s.shape[1] // HD)
            ],
            axis=1,
        )
        acc[part, :] += lax.dot_general(
            weights, value, NN, preferred_element_type=jnp.float32
        )

    def run(now, then):
        if then is not None:
            scores_then, top_then = then
            if first:
                pack(spans, own_v, got_v, v_ref, False)
            top_then[...] = jnp.broadcast_to(
                jnp.max(top_then[...], axis=1, keepdims=True), top_then.shape
            )
            acc[...] = jnp.zeros_like(acc)
        if now is not None:
            scores_now, top_now = now
            if first:
                pack(spans, own_k, got_k, k_ref, True)
            top_now[...] = jnp.full(top_now.shape, -3e38, jnp.float32)
            for start, q_ref in zip(starts, q_refs):
                q_all[start : start + q_ref.shape[0], :] = q_ref[...]

        def body(start, size):
            at = pl.ds(pl.multiple_of(start, UNIT), size)
            for part in parts:
                if now is not None:
                    score(at, scores_now, top_now, part)
                if then is not None:
                    weigh(at, scores_then, top_then, part)

        start = jnp.int32(0)
        for size in BLOCKS:
            turns = (count - start) // size

            @pl.loop(0, turns)
            def _(turn, start=start, size=size):
                body(start + turn * size, size)

            start = start + turns * size

        if then is not None:
            for b in range(blocks):
                finish(b, top_then)

    def finish(b, top):
        rows = q_refs[b].shape[0]
        index = lax.broadcasted_iota(jnp.int32, (stat_rows(rows), HD), 0)
        packed = jnp.zeros(index.shape, jnp.float32)
        for u, (start, size) in enumerate(groups_of(rows)):
            part = pl.ds(starts[b] + start, size)
            sums = acc[part, HD:]
            o_refs[b][start : start + size, :] = (acc[part, :HD] / sums).astype(jnp.bfloat16)
            logs = top[part, :] * SCALE + jnp.log2(sums)
            line = jnp.sum(jnp.where(eye_of(size), logs, 0.0), axis=0, keepdims=True)
            high = line.astype(jnp.bfloat16).astype(jnp.float32)
            middle = (line - high).astype(jnp.bfloat16).astype(jnp.float32)
            for i, term in enumerate((high, middle, line - high - middle)):
                packed = jnp.where(index == 3 * u + i, term, packed)
        o_refs[b][rows:, :] = packed.astype(jnp.bfloat16)

    even, odd = (s_even, top_even), (s_odd, top_odd)
    is_even = lax.rem(step, 2) == 0
    inside = jnp.logical_and(step > 0, step < tiles)

    @pl.when(step == 0)
    def _():
        mark(spans, passages, m_ref)
        run(even, None)

    if tiles > 1:

        @pl.when(jnp.logical_and(inside, is_even))
        def _():
            run(even, odd)

        @pl.when(jnp.logical_and(inside, jnp.logical_not(is_even)))
        def _():
            run(odd, even)

    @pl.when(step == tiles)
    def _():
        run(None, odd if tiles % 2 == 0 else even)


def attend(spans, meta, queries, raw, packed, after=()):
    first = packed is None
    blocks = len(queries)
    heights = [rows for _, _, rows in queries]
    tall = [rows + stat_rows(rows) for rows in heights]
    total = sum(heights)
    width = queries[0][0].shape[1]
    heads = width // HD
    tokens = raw[1].shape[0] if first else (packed[0].shape[1] - UNIT) // 2
    size = 2 * tokens + UNIT
    now = lambda t: jnp.minimum(t, heads - 1)
    then = lambda t: jnp.maximum(t - 1, 0)
    packed_specs = [
        pl.BlockSpec((None, size, HD), lambda t, n, g, m: (now(t), 0, 0)),
        pl.BlockSpec((None, size, HD), lambda t, n, g, m: (then(t), 0, 0)),
    ]
    raw_specs = [
        pl.BlockSpec((tokens, HD), lambda t, n, g, m: (0, m[0] * heads + now(t))),
        pl.BlockSpec((tokens, HD), lambda t, n, g, m: (0, now(t))),
        pl.BlockSpec((tokens, HD), lambda t, n, g, m: (0, m[0] * heads + then(t))),
        pl.BlockSpec((tokens, HD), lambda t, n, g, m: (0, then(t))),
    ]
    results = pl.pallas_call(
        functools.partial(attend_kernel, blocks, heads, first, len(after)),
        grid_spec=pltpu.PrefetchScalarGridSpec(
            num_scalar_prefetch=3,
            grid=(heads + 1,),
            in_specs=[
                pl.BlockSpec((rows, HD), lambda t, n, g, m, i=i: (i, now(t))) for _, i, rows in queries
            ]
            + (raw_specs if first else packed_specs)
            + [pl.BlockSpec(memory_space=pl.ANY)] * len(after),
            out_specs=[pl.BlockSpec((rows, HD), lambda t, n, g, m: (0, then(t))) for rows in tall]
            + (packed_specs if first else []),
            scratch_shapes=[
                pltpu.VMEM((total, HD), jnp.bfloat16),
                pltpu.VMEM((size, HD), jnp.bfloat16),
                pltpu.VMEM((total, size), jnp.float32),
                pltpu.VMEM((total, size), jnp.float32),
                pltpu.VMEM((total, HD), jnp.float32),
                pltpu.VMEM((total, HD), jnp.float32),
                pltpu.VMEM((total, 2 * HD), jnp.float32),
            ],
        ),
        out_shape=[jax.ShapeDtypeStruct((rows, width), jnp.bfloat16) for rows in tall]
        + [jax.ShapeDtypeStruct((heads, size, HD), jnp.bfloat16)] * (2 if first else 0),
        compiler_params=pltpu.CompilerParams(vmem_limit_bytes=VMEM),
        cost_estimate=pl.CostEstimate(
            flops=4 * total * size * width, bytes_accessed=4 * size * width, transcendentals=0
        ),
        name="attend",
    )(*spans, meta, *[x for x, _, _ in queries], *(raw if first else packed), *after)
    results = list(results)
    return results[:blocks], tuple(results[blocks:]) if first else packed


def merge_kernel(count, *refs):
    parts, (keep, give) = refs[:count], refs[-2:]
    half, width = keep.shape
    rows = 2 * half
    for u, (start, size) in enumerate(groups_of(rows)):
        eye = eye_of(size)
        out, there = (keep, start) if start < half else (give, start - half)
        for head in range(width // HD):
            cols = slice(head * HD, (head + 1) * HD)
            logs = []
            for part in parts:
                stats = part[rows:, cols].astype(jnp.float32)[3 * u : 3 * u + 3]
                logs.append(stats[0:1] + (stats[1:2] + stats[2:3]))
            most = functools.reduce(jnp.maximum, logs)
            shares = [jnp.exp2(x - most) for x in logs]
            whole = functools.reduce(jnp.add, shares)
            merged = None
            for part, share in zip(parts, shares):
                line = jnp.broadcast_to(share / whole, (size, HD))
                column = jnp.sum(jnp.where(eye, line, 0.0), axis=1, keepdims=True)
                term = part[start : start + size, cols].astype(jnp.float32) * column
                merged = term if merged is None else merged + term
            out[there : there + size, cols] = merged.astype(jnp.bfloat16)


def merge(parts, after=()):
    width = parts[0].shape[1]
    half = block_rows(parts[0].shape[0]) // 2
    shape = jax.ShapeDtypeStruct((half, width), jnp.bfloat16)
    return pl.pallas_call(
        functools.partial(merge_kernel, len(parts)),
        in_specs=[pl.BlockSpec(memory_space=pltpu.VMEM)] * len(parts)
        + [pl.BlockSpec(memory_space=pl.ANY)] * len(after),
        out_specs=[pl.BlockSpec(memory_space=pltpu.VMEM)] * 2,
        out_shape=[shape, shape],
        compiler_params=pltpu.CompilerParams(vmem_limit_bytes=MERGE_VMEM),
        cost_estimate=pl.CostEstimate(
            flops=0, bytes_accessed=4 * half * width * len(parts), transcendentals=0
        ),
        name="merge",
    )(*parts, *after)


def project_kernel(meta, keep, got, weight, *refs):
    groups = (len(refs) - 2) // 2
    outs, made, attended, done = refs[:groups], refs[groups : 2 * groups], refs[-2], refs[-1]
    width = keep.shape[1]
    cols = outs[0].shape[1]
    attended[:, pl.ds(pl.multiple_of(meta[0] * width, HD), width)] = keep[...]
    attended[:, pl.ds(pl.multiple_of((1 - meta[0]) * width, HD), width)] = got[...]
    order = list(reversed(range(groups)))
    copies = [pltpu.make_async_copy(made[d], outs[d], done.at[d]) for d in range(groups)]
    for d in order:
        at = pl.ds(pl.multiple_of((meta[1] ^ d) * cols, HD), cols)
        made[d][...] = lax.dot_general(
            attended[...], weight[:, at], NN, preferred_element_type=jnp.float32
        ).astype(made[d].dtype)
        copies[d].start()
    for d in order:
        copies[d].wait()


def project(meta, keep, got, out_weight, groups):
    depth, total = out_weight.shape
    rows, width = keep.shape
    cols = total // groups
    types = [jnp.float32] + [jnp.bfloat16] * (groups - 1)
    return pl.pallas_call(
        project_kernel,
        in_specs=[pl.BlockSpec(memory_space=pltpu.SMEM)]
        + [pl.BlockSpec(memory_space=pltpu.VMEM)] * 3,
        out_specs=[pl.BlockSpec(memory_space=pl.ANY)] * groups,
        scratch_shapes=[pltpu.VMEM((rows, cols), kind) for kind in types]
        + [pltpu.VMEM((rows, depth), jnp.bfloat16), pltpu.SemaphoreType.DMA((groups,))],
        out_shape=[jax.ShapeDtypeStruct((rows, cols), kind) for kind in types],
        compiler_params=pltpu.CompilerParams(vmem_limit_bytes=PROJECT_VMEM),
        cost_estimate=pl.CostEstimate(
            flops=2 * rows * depth * total, bytes_accessed=2 * depth * total, transcendentals=0
        ),
        name="project",
    )(meta, keep, got, out_weight)


def total_kernel(count, *refs):
    out = refs[-1]
    out[...] = refs[0][...] + sum(ref[...].astype(jnp.float32) for ref in refs[1:count])


def add_up(parts, start, total, before):
    rows, cols = parts[0].shape
    step = math.gcd(math.gcd(rows, start), 32)
    return pl.pallas_call(
        functools.partial(total_kernel, len(parts)),
        grid=(rows // step,),
        in_specs=[pl.BlockSpec((step, cols), lambda t: (t, 0))] * len(parts)
        + [pl.BlockSpec(memory_space=pl.ANY)] * len(before),
        out_specs=pl.BlockSpec((step, cols), lambda t: (start // step + t, 0)),
        out_shape=jax.ShapeDtypeStruct((total, cols), jnp.float32),
        input_output_aliases={len(parts): 0} if before else {},
        compiler_params=pltpu.CompilerParams(vmem_limit_bytes=MERGE_VMEM),
        cost_estimate=pl.CostEstimate(
            flops=0, bytes_accessed=2 * rows * cols * (len(parts) + 3), transcendentals=0
        ),
        name="add_up",
    )(*parts, *before)


def on_device(queries, keys, values, lengths, out_weight):
    sources = lax.axis_size("ctx")
    groups = lax.axis_size("head")
    core = lax.rem(lax.axis_index("ctx"), 2)
    width = keys.shape[1] // 2
    meta = jnp.stack([core, lax.axis_index("head")]).astype(jnp.int32)

    def swap(x, k, axis="ctx"):
        n = sources if axis == "ctx" else groups
        return lax.ppermute(x, axis, [(i, i ^ k) for i in range(n)])

    def half(x, which):
        return lax.dynamic_slice(x, (0, which * width), (x.shape[0], width))

    def others_of(x):
        return [swap(x, k) for k in reversed(range(2, sources, 2))]

    def back_to_owners(blocks):
        return [swap(block, k) for block, k in zip(blocks, reversed(range(2, sources, 2)))]

    def finish(parts, after=()):
        keep, give = merge(parts, after)
        return project(meta, keep, swap(give, 1), out_weight, groups)

    def arrive(blocks):
        far = [swap(blocks[d], d, "head") for d in reversed(range(1, groups))]
        return [blocks[0]] + far

    mine = half(queries, core)
    theirs = swap(half(queries, 1 - core), 1)
    keys_then, values_then, _ = lax.optimization_barrier((keys, values, theirs))
    got_k = swap(half(keys_then, 1 - core), 1)
    got_v = swap(half(values_then, 1 - core), 1)
    cuts = [0]
    for part in PARTS:
        cuts.append(cuts[-1] + queries.shape[0] * part // sum(PARTS))
    pairs = [x[cuts[i] : cuts[i + 1]] for i in range(3) for x in (mine, theirs)]
    early, late = jnp.concatenate(pairs[:2]), jnp.concatenate(pairs[2:])
    rows = [2 * (cuts[i + 1] - cuts[i]) for i in range(3)]
    asked = others_of(early)
    spans = (lengths, swap(lengths, 1))
    late, _ = lax.optimization_barrier((late, got_v))
    asked_late = others_of(late)

    raw = (keys, got_k, values, got_v)
    own, packed = attend(
        spans, meta, [(early, 0, rows[0]), (late, 0, rows[1]), (late, 1, rows[2])], raw, None
    )

    def others(x, index, size, after):
        partial, _ = attend(spans, meta, [(q, index, size) for q in x], raw, packed, after)
        return partial, back_to_owners(partial)

    done, back_0 = others(asked, 0, rows[0], ())
    done, back_1 = others(asked_late, 0, rows[1], done[:1])
    blocks_0 = finish(own[:1] + back_0, done[:1])
    done, back_2 = others(asked_late, 1, rows[2], blocks_0[:1])
    blocks_1 = finish(own[1:2] + back_1, done[:1])
    there_0 = arrive(blocks_0)
    blocks_1, there_0 = lax.optimization_barrier((blocks_1, there_0))
    there_1 = arrive(blocks_1)
    blocks_2 = finish(own[2:] + back_2, blocks_1[:1])
    there_2 = arrive(blocks_2)
    total = queries.shape[0]
    out = add_up(there_0, cuts[0], total, ())
    out = add_up(there_1, cuts[1], total, (out,))
    return add_up(there_2, cuts[2], total, (out,))


def solution(mesh):
    in_specs = (P("ctx", "head"), P("ctx", "head"), P("ctx", "head"), P("ctx"), P("head", None))
    out_specs = P("ctx", "head")
    return jax.shard_map(
        on_device, mesh=mesh, in_specs=in_specs, out_specs=out_specs, check_vma=False
    )
```

```python
import functools
import math

import jax
import jax.numpy as jnp
from jax import lax
from jax.experimental import pallas as pl
from jax.experimental.pallas import tpu as pltpu
from jax.sharding import PartitionSpec as P

HD = 128
SPAN = 256
STEP = 16
UNIT = 256
BLOCKS = (8 * UNIT, 3 * UNIT, 2 * UNIT, UNIT)
SUB = 256
PARTS = (2, 1, 1)
SCALE = math.log2(math.e) / math.sqrt(HD)
NT = (((1,), (1,)), ((), ()))
NN = (((1,), (0,)), ((), ()))
MIB = 2**20
VMEM = 50 * MIB
MERGE_VMEM = 12 * MIB
PROJECT_VMEM = 16 * MIB


def groups_of(rows):
    half = rows // 2
    size = min(half, HD)
    return [
        (core * half + at, min(size, half - at)) for core in range(2) for at in range(0, half, size)
    ]


def stat_rows(rows):
    return (3 * len(groups_of(rows)) + 15) // 16 * 16


def block_rows(tall):
    return next(rows for rows in range(32, tall, 32) if rows + stat_rows(rows) == tall)


def eye_of(size):
    return lax.broadcasted_iota(jnp.int32, (size, HD), 0) == (
        lax.broadcasted_iota(jnp.int32, (size, HD), 1)
    )


def round_up(size):
    return (size + STEP - 1) // STEP * STEP


def pack(spans, own, got, out, fill):
    here = own.shape[0] // SPAN
    rows = lax.broadcasted_iota(jnp.int32, (STEP, HD), 0)
    at = jnp.int32(0)
    for passage in range(2 * here):
        source = own if passage < here else got
        base = passage % here * SPAN
        size = spans[passage]
        out[pl.ds(pl.multiple_of(at, STEP), SPAN), :] = source[base : base + SPAN, :]
        edge = jnp.minimum(size // STEP * STEP, SPAN - STEP)
        last = source[pl.ds(pl.multiple_of(base + edge, STEP), STEP), :].astype(jnp.float32)
        if fill:
            filler = jnp.broadcast_to(
                source[base : base + STEP, :].astype(jnp.float32)[:1, :], (STEP, HD)
            )
        else:
            filler = jnp.zeros((STEP, HD), jnp.float32)
        out[pl.ds(pl.multiple_of(at + edge, STEP), STEP), :] = jnp.where(
            rows + edge < size, last, filler
        ).astype(jnp.bfloat16)
        at = at + round_up(size)
    filler = filler.astype(jnp.bfloat16)
    for i in range(UNIT // STEP):
        out[pl.ds(pl.multiple_of(at + i * STEP, STEP), STEP), :] = filler


def mark(spans, passages, out):
    rows = lax.broadcasted_iota(jnp.int32, (STEP, HD), 0)
    at = jnp.int32(0)
    for passage in range(passages):
        size = spans[passage]
        out[pl.ds(pl.multiple_of(at, STEP), SPAN), :] = jnp.ones((SPAN, HD), jnp.bfloat16)
        edge = jnp.minimum(size // STEP * STEP, SPAN - STEP)
        out[pl.ds(pl.multiple_of(at + edge, STEP), STEP), :] = jnp.where(
            rows + edge < size, 1.0, 0.0
        ).astype(jnp.bfloat16)
        at = at + round_up(size)
    out[pl.ds(pl.multiple_of(at, STEP), UNIT), :] = jnp.zeros((UNIT, HD), jnp.bfloat16)


def attend_kernel(blocks, tiles, first, afters, own_spans, got_spans, meta, *refs):
    here = own_spans.shape[0]
    spans = [own_spans[i] for i in range(here)] + [got_spans[i] for i in range(here)]
    refs = list(refs)
    take = lambda n: [refs.pop(0) for _ in range(n)]
    q_refs = take(blocks)
    if first:
        own_k, got_k, own_v, got_v = take(4)
    else:
        k_ref, v_ref = take(2)
    take(afters)
    o_refs = take(blocks)
    if first:
        k_ref, v_ref = take(2)
    q_all, m_ref, s_even, s_odd, top_even, top_odd, acc = refs
    starts, total = [], 0
    for q_ref in q_refs:
        starts.append(total)
        total += q_ref.shape[0]
    step = pl.program_id(0)
    passages = (k_ref.shape[0] - UNIT) // SPAN
    count = sum(round_up(spans[i]) for i in range(passages))
    count = (count + UNIT - 1) // UNIT * UNIT
    parts = [pl.ds(r, min(SUB, total - r)) for r in range(0, total, SUB)]

    def score(at, scores, top, part):
        s = lax.dot_general(
            q_all[part, :], k_ref[at, :], NT, preferred_element_type=jnp.float32
        )
        scores[part, at] = s
        most = top[part, :]
        for i in range(s.shape[1] // HD):
            most = jnp.maximum(most, s[:, i * HD : (i + 1) * HD])
        top[part, :] = most

    def weigh(at, scores, top, part):
        value = jnp.concatenate([v_ref[at, :], m_ref[at, :]], axis=1)
        most = top[part, :]
        s = scores[part, at]
        weights = jnp.concatenate(
            [
                jnp.exp2((s[:, i * HD : (i + 1) * HD] - most) * SCALE).astype(jnp.bfloat16)
                for i in range(s.shape[1] // HD)
            ],
            axis=1,
        )
        acc[part, :] += lax.dot_general(
            weights, value, NN, preferred_element_type=jnp.float32
        )

    def run(now, then):
        if then is not None:
            scores_then, top_then = then
            if first:
                pack(spans, own_v, got_v, v_ref, False)
            top_then[...] = jnp.broadcast_to(
                jnp.max(top_then[...], axis=1, keepdims=True), top_then.shape
            )
            acc[...] = jnp.zeros_like(acc)
        if now is not None:
            scores_now, top_now = now
            if first:
                pack(spans, own_k, got_k, k_ref, True)
            top_now[...] = jnp.full(top_now.shape, -3e38, jnp.float32)
            for start, q_ref in zip(starts, q_refs):
                q_all[start : start + q_ref.shape[0], :] = q_ref[...]

        def body(start, size):
            at = pl.ds(pl.multiple_of(start, UNIT), size)
            for part in parts:
                if now is not None:
                    score(at, scores_now, top_now, part)
                if then is not None:
                    weigh(at, scores_then, top_then, part)

        start = jnp.int32(0)
        for size in BLOCKS:
            turns = (count - start) // size

            @pl.loop(0, turns)
            def _(turn, start=start, size=size):
                body(start + turn * size, size)

            start = start + turns * size

        if then is not None:
            for b in range(blocks):
                finish(b, top_then)

    def finish(b, top):
        rows = q_refs[b].shape[0]
        index = lax.broadcasted_iota(jnp.int32, (stat_rows(rows), HD), 0)
        packed = jnp.zeros(index.shape, jnp.float32)
        for u, (start, size) in enumerate(groups_of(rows)):
            part = pl.ds(starts[b] + start, size)
            sums = acc[part, HD:]
            o_refs[b][start : start + size, :] = (acc[part, :HD] / sums).astype(jnp.bfloat16)
            logs = top[part, :] * SCALE + jnp.log2(sums)
            line = jnp.sum(jnp.where(eye_of(size), logs, 0.0), axis=0, keepdims=True)
            high = line.astype(jnp.bfloat16).astype(jnp.float32)
            middle = (line - high).astype(jnp.bfloat16).astype(jnp.float32)
            for i, term in enumerate((high, middle, line - high - middle)):
                packed = jnp.where(index == 3 * u + i, term, packed)
        o_refs[b][rows:, :] = packed.astype(jnp.bfloat16)

    even, odd = (s_even, top_even), (s_odd, top_odd)
    is_even = lax.rem(step, 2) == 0
    inside = jnp.logical_and(step > 0, step < tiles)

    @pl.when(step == 0)
    def _():
        mark(spans, passages, m_ref)
        run(even, None)

    if tiles > 1:

        @pl.when(jnp.logical_and(inside, is_even))
        def _():
            run(even, odd)

        @pl.when(jnp.logical_and(inside, jnp.logical_not(is_even)))
        def _():
            run(odd, even)

    @pl.when(step == tiles)
    def _():
        run(None, odd if tiles % 2 == 0 else even)


def attend(spans, meta, queries, raw, packed, after=()):
    first = packed is None
    blocks = len(queries)
    heights = [rows for _, _, rows in queries]
    tall = [rows + stat_rows(rows) for rows in heights]
    total = sum(heights)
    width = queries[0][0].shape[1]
    heads = width // HD
    tokens = raw[1].shape[0] if first else (packed[0].shape[1] - UNIT) // 2
    size = 2 * tokens + UNIT
    now = lambda t: jnp.minimum(t, heads - 1)
    then = lambda t: jnp.maximum(t - 1, 0)
    packed_specs = [
        pl.BlockSpec((None, size, HD), lambda t, n, g, m: (now(t), 0, 0)),
        pl.BlockSpec((None, size, HD), lambda t, n, g, m: (then(t), 0, 0)),
    ]
    raw_specs = [
        pl.BlockSpec((tokens, HD), lambda t, n, g, m: (0, m[0] * heads + now(t))),
        pl.BlockSpec((tokens, HD), lambda t, n, g, m: (0, now(t))),
        pl.BlockSpec((tokens, HD), lambda t, n, g, m: (0, m[0] * heads + then(t))),
        pl.BlockSpec((tokens, HD), lambda t, n, g, m: (0, then(t))),
    ]
    results = pl.pallas_call(
        functools.partial(attend_kernel, blocks, heads, first, len(after)),
        grid_spec=pltpu.PrefetchScalarGridSpec(
            num_scalar_prefetch=3,
            grid=(heads + 1,),
            in_specs=[
                pl.BlockSpec((rows, HD), lambda t, n, g, m, i=i: (i, now(t))) for _, i, rows in queries
            ]
            + (raw_specs if first else packed_specs)
            + [pl.BlockSpec(memory_space=pl.ANY)] * len(after),
            out_specs=[pl.BlockSpec((rows, HD), lambda t, n, g, m: (0, then(t))) for rows in tall]
            + (packed_specs if first else []),
            scratch_shapes=[
                pltpu.VMEM((total, HD), jnp.bfloat16),
                pltpu.VMEM((size, HD), jnp.bfloat16),
                pltpu.VMEM((total, size), jnp.float32),
                pltpu.VMEM((total, size), jnp.float32),
                pltpu.VMEM((total, HD), jnp.float32),
                pltpu.VMEM((total, HD), jnp.float32),
                pltpu.VMEM((total, 2 * HD), jnp.float32),
            ],
        ),
        out_shape=[jax.ShapeDtypeStruct((rows, width), jnp.bfloat16) for rows in tall]
        + [jax.ShapeDtypeStruct((heads, size, HD), jnp.bfloat16)] * (2 if first else 0),
        compiler_params=pltpu.CompilerParams(vmem_limit_bytes=VMEM),
        cost_estimate=pl.CostEstimate(
            flops=4 * total * size * width, bytes_accessed=4 * size * width, transcendentals=0
        ),
        name="attend",
    )(*spans, meta, *[x for x, _, _ in queries], *(raw if first else packed), *after)
    results = list(results)
    return results[:blocks], tuple(results[blocks:]) if first else packed


def merge_kernel(count, *refs):
    parts, (keep, give) = refs[:count], refs[-2:]
    half, width = keep.shape
    rows = 2 * half
    for u, (start, size) in enumerate(groups_of(rows)):
        eye = eye_of(size)
        out, there = (keep, start) if start < half else (give, start - half)
        for head in range(width // HD):
            cols = slice(head * HD, (head + 1) * HD)
            logs = []
            for part in parts:
                stats = part[rows:, cols].astype(jnp.float32)[3 * u : 3 * u + 3]
                logs.append(stats[0:1] + (stats[1:2] + stats[2:3]))
            most = functools.reduce(jnp.maximum, logs)
            shares = [jnp.exp2(x - most) for x in logs]
            whole = functools.reduce(jnp.add, shares)
            merged = None
            for part, share in zip(parts, shares):
                line = jnp.broadcast_to(share / whole, (size, HD))
                column = jnp.sum(jnp.where(eye, line, 0.0), axis=1, keepdims=True)
                term = part[start : start + size, cols].astype(jnp.float32) * column
                merged = term if merged is None else merged + term
            out[there : there + size, cols] = merged.astype(jnp.bfloat16)


def merge(parts, after=()):
    width = parts[0].shape[1]
    half = block_rows(parts[0].shape[0]) // 2
    shape = jax.ShapeDtypeStruct((half, width), jnp.bfloat16)
    return pl.pallas_call(
        functools.partial(merge_kernel, len(parts)),
        in_specs=[pl.BlockSpec(memory_space=pltpu.VMEM)] * len(parts)
        + [pl.BlockSpec(memory_space=pl.ANY)] * len(after),
        out_specs=[pl.BlockSpec(memory_space=pltpu.VMEM)] * 2,
        out_shape=[shape, shape],
        compiler_params=pltpu.CompilerParams(vmem_limit_bytes=MERGE_VMEM),
        cost_estimate=pl.CostEstimate(
            flops=0, bytes_accessed=4 * half * width * len(parts), transcendentals=0
        ),
        name="merge",
    )(*parts, *after)


def project_kernel(meta, keep, got, weight, *refs):
    outs, attended = refs[:-1], refs[-1]
    width = keep.shape[1]
    cols = outs[0].shape[1]
    attended[:, pl.ds(pl.multiple_of(meta[0] * width, HD), width)] = keep[...]
    attended[:, pl.ds(pl.multiple_of((1 - meta[0]) * width, HD), width)] = got[...]
    for d, out in enumerate(outs):
        at = pl.ds(pl.multiple_of((meta[1] ^ d) * cols, HD), cols)
        out[...] = lax.dot_general(
            attended[...], weight[:, at], NN, preferred_element_type=jnp.float32
        ).astype(out.dtype)


def project(meta, keep, got, out_weight, groups):
    depth, total = out_weight.shape
    rows, width = keep.shape
    cols = total // groups
    types = [jnp.float32] + [jnp.bfloat16] * (groups - 1)
    return pl.pallas_call(
        project_kernel,
        in_specs=[pl.BlockSpec(memory_space=pltpu.SMEM)]
        + [pl.BlockSpec(memory_space=pltpu.VMEM)] * 3,
        out_specs=[pl.BlockSpec(memory_space=pltpu.VMEM)] * groups,
        scratch_shapes=[pltpu.VMEM((rows, depth), jnp.bfloat16)],
        out_shape=[jax.ShapeDtypeStruct((rows, cols), kind) for kind in types],
        compiler_params=pltpu.CompilerParams(vmem_limit_bytes=PROJECT_VMEM),
        cost_estimate=pl.CostEstimate(
            flops=2 * rows * depth * total, bytes_accessed=2 * depth * total, transcendentals=0
        ),
        name="project",
    )(meta, keep, got, out_weight)


def total_kernel(count, *refs):
    out = refs[-1]
    out[...] = refs[0][...] + sum(ref[...].astype(jnp.float32) for ref in refs[1:count])


def add_up(parts, start, total, before):
    rows, cols = parts[0].shape
    step = math.gcd(math.gcd(rows, start), 32)
    return pl.pallas_call(
        functools.partial(total_kernel, len(parts)),
        grid=(rows // step,),
        in_specs=[pl.BlockSpec((step, cols), lambda t: (t, 0))] * len(parts)
        + [pl.BlockSpec(memory_space=pl.ANY)] * len(before),
        out_specs=pl.BlockSpec((step, cols), lambda t: (start // step + t, 0)),
        out_shape=jax.ShapeDtypeStruct((total, cols), jnp.float32),
        input_output_aliases={len(parts): 0} if before else {},
        compiler_params=pltpu.CompilerParams(vmem_limit_bytes=MERGE_VMEM),
        cost_estimate=pl.CostEstimate(
            flops=0, bytes_accessed=2 * rows * cols * (len(parts) + 3), transcendentals=0
        ),
        name="add_up",
    )(*parts, *before)


def on_device(queries, keys, values, lengths, out_weight):
    sources = lax.axis_size("ctx")
    groups = lax.axis_size("head")
    core = lax.rem(lax.axis_index("ctx"), 2)
    width = keys.shape[1] // 2
    meta = jnp.stack([core, lax.axis_index("head")]).astype(jnp.int32)

    def swap(x, k, axis="ctx"):
        n = sources if axis == "ctx" else groups
        return lax.ppermute(x, axis, [(i, i ^ k) for i in range(n)])

    def half(x, which):
        return lax.dynamic_slice(x, (0, which * width), (x.shape[0], width))

    def others_of(x):
        return [swap(x, k) for k in reversed(range(2, sources, 2))]

    def back_to_owners(blocks):
        return [swap(block, k) for block, k in zip(blocks, reversed(range(2, sources, 2)))]

    def finish(parts, after=()):
        keep, give = merge(parts, after)
        return project(meta, keep, swap(give, 1), out_weight, groups)

    def arrive(blocks):
        far = [swap(blocks[d], d, "head") for d in reversed(range(1, groups))]
        return [blocks[0]] + far

    mine = half(queries, core)
    theirs = swap(half(queries, 1 - core), 1)
    keys_then, values_then, _ = lax.optimization_barrier((keys, values, theirs))
    got_k = swap(half(keys_then, 1 - core), 1)
    got_v = swap(half(values_then, 1 - core), 1)
    cuts = [0]
    for part in PARTS:
        cuts.append(cuts[-1] + queries.shape[0] * part // sum(PARTS))
    pairs = [x[cuts[i] : cuts[i + 1]] for i in range(3) for x in (mine, theirs)]
    early, late = jnp.concatenate(pairs[:2]), jnp.concatenate(pairs[2:])
    rows = [2 * (cuts[i + 1] - cuts[i]) for i in range(3)]
    asked = others_of(early)
    spans = (lengths, swap(lengths, 1))
    late, _ = lax.optimization_barrier((late, got_v))
    asked_late = others_of(late)

    raw = (keys, got_k, values, got_v)
    own, packed = attend(
        spans, meta, [(early, 0, rows[0]), (late, 0, rows[1]), (late, 1, rows[2])], raw, None
    )

    def others(x, index, size, after):
        partial, _ = attend(spans, meta, [(q, index, size) for q in x], raw, packed, after)
        return partial, back_to_owners(partial)

    done, back_0 = others(asked, 0, rows[0], ())
    done, back_1 = others(asked_late, 0, rows[1], done[:1])
    blocks_0 = finish(own[:1] + back_0, done[:1])
    done, back_2 = others(asked_late, 1, rows[2], blocks_0[:1])
    blocks_1 = finish(own[1:2] + back_1, done[:1])
    there_0 = arrive(blocks_0)
    blocks_1, there_0 = lax.optimization_barrier((blocks_1, there_0))
    there_1 = arrive(blocks_1)
    blocks_2 = finish(own[2:] + back_2, blocks_1[:1])
    there_2 = arrive(blocks_2)
    total = queries.shape[0]
    out = add_up(there_0, cuts[0], total, ())
    out = add_up(there_1, cuts[1], total, (out,))
    return add_up(there_2, cuts[2], total, (out,))


def solution(mesh):
    in_specs = (P("ctx", "head"), P("ctx", "head"), P("ctx", "head"), P("ctx"), P("head", None))
    out_specs = P("ctx", "head")
    return jax.shard_map(
        on_device, mesh=mesh, in_specs=in_specs, out_specs=out_specs, check_vma=False
    )
```
